128 devices in a mesh: dp: 4 (over z_lo, core), context: 16 (over y, x), tensor: 2 (over z_hi).
Axes of the slice: x: 4, y: 4, z: 4 (z_hi: 2, z_lo: 2; z = z_hi * 2 + z_lo), core: 2. Of those that a mesh axis runs over, the one named last changes fastest.
Arguments:
- queries: bfloat16 [24576, 2048], P(('dp', 'context'), 'tensor'), parts along dimension 0, may hold values from -256 to 256
- keys: bfloat16 [24576, 2048], P(('dp', 'context'), 'tensor'), parts along dimension 0, may hold values from -256 to 256
- values: bfloat16 [24576, 2048], P(('dp', 'context'), 'tensor'), parts along dimension 0, may hold values from -6 to 6
- out_weight: bfloat16 [2048, 4096], P('tensor'), may hold values from -0.125 to 0.125
- doc_lengths: int32 [24], P('dp'), parts along dimension 0, may hold values from 1 to 1536, 6144 in all
- spans: int32 [124, 2], P('dp'), parts along dimension 0, may hold values from 0 to 6144, as said below
- assignment: int32 [192], P('dp'), parts along dimension 0, may hold values from 0 to 47, each once
Outputs:
- mixed: bfloat16 [24576, 4096], P(('dp', 'context', 'tensor')), parts along dimension 0
The draws below stay inside these ranges and needn't reach their ends.
There are 4 independent parts, one for each index of `dp`. The reference program is written for one: setup_inputs(seed, part) draws one part's arguments, and reference() takes and returns one part's arrays. A program takes and returns all parts, laid end to end along the dimension named above; an argument that names none is the same for every part. Nothing has to cross between parts.
Inputs may be any that keep to these rules, and one draw needn't show every extreme that they name: `doc_lengths`: they sum to 6144. Each row is a span [start, end) with start < end; spans are disjoint and in increasing order; each holds at most 198 positions, and one holds exactly that many. `assignment`: a permutation of the query blocks.
All inputs are finite; a program needn't handle non-finite values.
Results may differ from the reference program's by a relative error of at most 0.013.
Values may be sent and summed in bfloat16 or wider, within the bound.
No kernel may reach another device: no remote copies, remote signals or barrier semaphores. Data moves between devices by JAX's collectives and lax.ppermute only.
A program may use at most 128 MiB of HBM per device.

```python
import math
import jax
import jax.numpy as jnp
import numpy as np
from jax import lax

D = 4096
HEADS = 16
HD = 128
QB = 128
NDOC = 6
SEQ = 6144
NBLK = 48
NSPAN = 31
DOCMAX = 1536


def shared_normals(key):
    first_key, second_key = jax.random.split(key)
    key_base = jax.random.normal(first_key, (SEQ, HEADS * HD), jnp.float32)
    query_base = jax.random.normal(second_key, (SEQ, HEADS * HD), jnp.float32)
    return (key_base, query_base)


def draw_keys(key, part):
    key_base, query_base = shared_normals(key)
    return key_base.astype(jnp.bfloat16)


def draw_queries(key, part):
    key_base, query_base = shared_normals(key)
    return query_base.astype(jnp.bfloat16)


def draw_spans(key, part):
    key = jax.random.fold_in(key, 7)
    first_key, second_key = jax.random.split(key)
    slot_len = SEQ // NSPAN
    span_len = jax.random.randint(first_key, (NSPAN,), slot_len // 4, slot_len + 1)
    span_len = jnp.where(jnp.arange(NSPAN, dtype=jnp.int32) == 0, slot_len, span_len)
    offsets = jax.random.randint(second_key, (NSPAN,), 0, 1048576) % (slot_len - span_len + 1)
    starts = jnp.arange(NSPAN, dtype=jnp.int32) * slot_len + offsets
    return jnp.stack([starts, starts + span_len], axis=1).astype(jnp.int32)


def level_of(rng, shape, cuts, least, largest):
    factor_of = 1.0
    for position, shards_of in cuts:
        heights = jax.random.uniform(jax.random.fold_in(jax.random.fold_in(rng, 6), position), (shards_of,), jnp.float32, least / len(cuts), largest / len(cuts))
        factor_of = factor_of * jnp.repeat(jnp.exp(heights), shape[position] // shards_of).reshape((-1,) + (1,) * (len(shape) - 1 - position))
    return factor_of


def length_profile(amount, total, bound, skew):
    portions = [(1 << 20) // math.isqrt(standing ** skew) + 1 for standing in range(2, amount + 1)]
    surplus, holding = total - bound - (amount - 1), [1] * (amount - 1)
    while surplus > 0:
        free = [i for i in range(amount - 1) if holding[i] < bound]
        whole, remaining = sum([portions[i] for i in free]), surplus
        for i in free:
            addition = min(bound - holding[i], max(1, remaining * portions[i] // whole), surplus)
            holding[i] = holding[i] + addition
            surplus = surplus - addition
    return np.array([bound] + holding)


def uneven_parts(own_key, count, total, limit, skew):
    if count == 2:
        one = jax.random.randint(own_key, (), max(1, total - limit), min(limit, total - 1) + 1)
        return jnp.stack([one, total - one])
    lengths = jnp.asarray(length_profile(count, total, limit, skew), jnp.int32)
    pairs = (count - 1) // 2
    donor, taker = lengths[1:1 + 2 * pairs:2], lengths[2:2 + 2 * pairs:2]
    room = jnp.minimum(donor - 1, limit - taker)
    passed = jax.random.randint(jax.random.fold_in(own_key, 1), (pairs,), 0, 1 << 20) % (room + 1)
    lengths = lengths.at[1:1 + 2 * pairs:2].set(donor - passed).at[2:2 + 2 * pairs:2].set(taker + passed)
    return lengths[jax.random.permutation(jax.random.fold_in(own_key, 2), count)]


def bell_draw(own_key, shape, spread, limit, pieces=(), kind=jnp.bfloat16):
    values = jax.random.normal(own_key, shape, jnp.float32) * spread
    if len(pieces) > 0:
        values = level_of(own_key, shape, pieces, -0.22, 0.18) * values
    return jnp.clip(values, min=-limit, max=limit).astype(kind)


def setup_inputs(seed: int = 0, part: int = 0) -> dict:
    streams_of = jax.random.split(jax.random.key(seed), 8)
    part_splits = jax.random.split(jax.random.fold_in(streams_of[7], part), 8)
    queries = draw_queries(jax.random.fold_in(jax.random.fold_in(streams_of[7], part), 71), part)
    keys = draw_keys(jax.random.fold_in(jax.random.fold_in(streams_of[7], part), 71), part)
    values = bell_draw(part_splits[2], (SEQ, HEADS * HD), 1.0, 6.0, ((0, 16), (1, 2)))
    out_weight = bell_draw(streams_of[3], (HEADS * HD, D), (HEADS * HD) ** -0.5, 0.125, ((0, 2),))
    doc_lengths = uneven_parts(part_splits[4], NDOC, SEQ, DOCMAX, 2).astype(jnp.int32)
    spans = draw_spans(jax.random.fold_in(jax.random.fold_in(streams_of[7], part), 71), part)
    assignment = jax.random.permutation(part_splits[6], NBLK).astype(jnp.int32)
    return {"queries": queries, "keys": keys, "values": values, "out_weight": out_weight, "doc_lengths": doc_lengths, "spans": spans, "assignment": assignment}


def document_index(positions, doc_lengths):
    bounds = jnp.cumsum(doc_lengths).astype(jnp.int32)[:-1]
    return lax.optimization_barrier(jnp.sum((positions[:, None] >= bounds[None, :]).astype(jnp.int32), axis=1)).astype(jnp.int32)

def span_index(positions, spans):
    inside = (positions[:, None] >= spans[None, :, 0]) & (positions[:, None] < spans[None, :, 1])
    labels = jnp.arange(1, spans.shape[0] + 1, dtype=jnp.int32)
    return (lax.optimization_barrier(jnp.sum(jnp.where(inside, labels[None, :], 0), axis=1)) - 1).astype(jnp.int32)

def visible(query_pos, key_pos, doc_lengths, spans, seq_total):
    query_doc = document_index(query_pos, doc_lengths)
    key_doc = document_index(key_pos, doc_lengths)
    query_span = span_index(query_pos, spans)
    key_span = span_index(key_pos, spans)
    same_doc = query_doc[:, None] == key_doc[None, :]
    earlier = key_pos[None, :] <= query_pos[:, None]
    same_span = (query_span[:, None] == key_span[None, :]) & (query_span[:, None] >= 0)
    in_range = (key_pos >= 0) & (key_pos < seq_total)
    return same_doc & (earlier | same_span) & in_range[None, :]

def reference(queries, keys, values, out_weight, doc_lengths, spans, assignment):
    positions = jnp.arange(SEQ, dtype=jnp.int32)
    allowed = visible(positions, positions, doc_lengths, spans, SEQ)
    features = HEADS * HD
    scale = 1.0 / math.sqrt(HD)

    def one_head(head):
        query_head = lax.dynamic_slice_in_dim(queries, head * HD, HD, 1)
        key_head = lax.dynamic_slice_in_dim(keys, head * HD, HD, 1)
        value_head = lax.dynamic_slice_in_dim(values, head * HD, HD, 1)
        scores = jnp.dot(query_head, key_head.T, preferred_element_type=jnp.float32) * scale
        scores = jnp.where(allowed, scores, -1e+30)
        highest = lax.optimization_barrier(jnp.max(scores, axis=1, keepdims=True))
        weights = jnp.where(allowed, jnp.exp(scores - highest), 0.0)
        denominator = lax.optimization_barrier(jnp.sum(weights, axis=1, keepdims=True))
        summed = jnp.dot(weights.astype(jnp.bfloat16), value_head, preferred_element_type=jnp.float32)
        return summed / denominator
    per_head = lax.map(one_head, jnp.arange(HEADS, dtype=jnp.int32))
    attended = jnp.transpose(per_head, (1, 0, 2)).reshape(SEQ, features).astype(jnp.bfloat16)
    owned = attended.reshape(NBLK, QB, features)[assignment].reshape(SEQ, features)
    return jnp.dot(owned, out_weight, preferred_element_type=jnp.float32).astype(jnp.bfloat16)
```

```python
import functools
import math

import jax
import jax.numpy as jnp
from jax import lax
from jax.experimental import pallas as pl
from jax.experimental.pallas import tpu as pltpu
from jax.sharding import Mesh, PartitionSpec as P

HD = 128
QB = 128
QTR = QB // 4
HALF = QB // 2
NCTX = 16
CHIP_BLOCKS = 3
NBLK = NCTX * CHIP_BLOCKS
HEADS = 8
ROWS = NBLK * HALF
NDOC = 6
NSPAN = 31
TILE = 4
TROWS = TILE * HALF
TPOS = TILE * QB
NTILE = NBLK // TILE
SCALE2 = math.log2(math.e) / math.sqrt(HD)
NEG = -1e30
BF = jnp.bfloat16
F32 = jnp.float32


def pack_kernel(core_ref, q_ref, k_ref, v_ref, own_ref, send_ref):
    core = core_ref[0]
    for out_ref, parity in ((own_ref, core), (send_ref, 1 - core)):
        for a, ref in enumerate((q_ref, k_ref, v_ref)):
            for group in range(2 * CHIP_BLOCKS):
                start = pl.multiple_of(group * HALF + parity * QTR, QTR)
                rows = ref[pl.ds(start, QTR), :]
                for h in range(HEADS):
                    out_ref[h, group * QTR : (group + 1) * QTR, a * HD : (a + 1) * HD] = rows[
                        :, h * HD : (h + 1) * HD
                    ]


def pack(core, q, k, v):
    out = jax.ShapeDtypeStruct((HEADS, CHIP_BLOCKS * HALF, 3 * HD), BF)
    vmem = pl.BlockSpec(memory_space=pltpu.VMEM)
    return pl.pallas_call(
        pack_kernel,
        out_shape=(out, out),
        in_specs=[pl.BlockSpec(memory_space=pltpu.SMEM), vmem, vmem, vmem],
        out_specs=(vmem, vmem),
        compiler_params=pltpu.CompilerParams(vmem_limit_bytes=32 << 20),
        name="pack",
    )(core, q, k, v)


def attend_kernel(ints_ref, y_ref, kvo_ref, o_ref, inv_ref):
    core = ints_ref[0]
    spans_at = 1 + NDOC
    assign_at = spans_at + 2 * NSPAN

    def invert(j, c):
        inv_ref[ints_ref[assign_at + j]] = j
        return c

    lax.fori_loop(0, NBLK, invert, 0)

    def half_pos(index, parity):
        return (index // HALF) * QB + ((index // QTR) % 2) * HALF + parity * QTR + index % QTR

    def query_tile(j, c):
        first = j * TPOS
        pos = half_pos(lax.broadcasted_iota(jnp.int32, (8, TROWS), 1), core) + first
        lo = jnp.zeros_like(pos)
        doc_end = jnp.full_like(pos, ints_ref[1])
        lo_first = jnp.int32(0)
        start = jnp.int32(0)
        for d in range(NDOC):
            end = start + ints_ref[1 + d]
            here = pos >= start
            lo = jnp.where(here, start, lo)
            doc_end = jnp.where(here, end, doc_end)
            lo_first = jnp.where(first >= start, start, lo_first)
            start = end

        def one_span(s, hi):
            a = ints_ref[spans_at + 2 * s]
            b = ints_ref[spans_at + 2 * s + 1]
            return jnp.where((pos >= a) & (pos < b), b, hi)

        hi = lax.fori_loop(0, NSPAN, one_span, pos + 1, unroll=True)
        hi = jnp.minimum(hi, doc_end)
        hi_last = jnp.max(hi)
        lo = lo[:1]
        hi = hi[:1]
        q = y_ref[pl.ds(pl.multiple_of(j * TROWS, TROWS), TROWS), :HD]
        key_iota = half_pos(lax.broadcasted_iota(jnp.int32, (TROWS, TROWS), 0), 0)

        def key_tile(t, carry):
            m, l, acc = carry
            rows = pl.ds(pl.multiple_of(t * TROWS, TROWS), TROWS)
            parts = (
                (y_ref[rows, HD : 2 * HD], y_ref[rows, 2 * HD :], core),
                (kvo_ref[rows, :HD], kvo_ref[rows, HD:], 1 - core),
            )
            scores = []
            for key, _, parity in parts:
                s = lax.dot_general(
                    key, q, (((1,), (1,)), ((), ())), preferred_element_type=F32
                ) * SCALE2
                base = t * TPOS + parity * QTR
                s = jnp.where((key_iota >= lo - base) & (key_iota < hi - base), s, NEG)
                scores.append(s)
            peak = jnp.maximum(
                jnp.max(scores[0], axis=0, keepdims=True), jnp.max(scores[1], axis=0, keepdims=True)
            )
            new_m = jnp.maximum(m, peak)
            factor = jnp.exp2(m - new_m)
            l = l * factor
            acc = acc * factor
            for s, (_, value, _) in zip(scores, parts):
                p = jnp.exp2(s - new_m)
                l = l + jnp.sum(p, axis=0, keepdims=True)
                acc = acc + lax.dot_general(
                    value, p.astype(BF), (((0,), (0,)), ((), ())), preferred_element_type=F32
                )
            return new_m, l, acc

        _, l, acc = lax.fori_loop(
            lo_first // TPOS,
            (hi_last + (TPOS - 1)) // TPOS,
            key_tile,
            (
                jnp.full((1, TROWS), NEG, F32),
                jnp.zeros((1, TROWS), F32),
                jnp.zeros((HD, TROWS), F32),
            ),
        )
        out = jnp.transpose(acc / l).astype(BF)
        for b in range(TILE):
            slot = inv_ref[j * TILE + b]
            chip = slot // CHIP_BLOCKS
            for u in range(2):
                group = (slot % CHIP_BLOCKS) * 2 + u
                o_ref[group // 3, chip, group % 3] = out[
                    b * HALF + u * QTR : b * HALF + (u + 1) * QTR
                ]
        return c

    lax.fori_loop(0, NTILE, query_tile, 0)


def attend(ints, y, kvo):
    vmem = pl.BlockSpec(memory_space=pltpu.VMEM)
    return pl.pallas_call(
        attend_kernel,
        out_shape=jax.ShapeDtypeStruct((2, NCTX, 3, QTR, HD), BF),
        in_specs=[pl.BlockSpec(memory_space=pltpu.SMEM), vmem, vmem],
        out_specs=vmem,
        scratch_shapes=[pltpu.SMEM((NBLK,), jnp.int32)],
        compiler_params=pltpu.CompilerParams(vmem_limit_bytes=32 << 20),
        name="attend",
    )(ints, y, kvo)


COLS = 512


def project_kernel(ids_ref, z_ref, zo_ref, w_ref, wf_ref, wr_ref, o_ref, a_ref):
    core = ids_ref[0]
    t_own = ids_ref[1]

    @pl.when(pl.program_id(0) == 0)
    def _():
        for side in range(2):
            src = t_own if side == 0 else 1 - t_own
            for n in range(HEADS):
                h = n if side == 0 else lax.rem(n + core * (HEADS // 2), HEADS)
                col = pl.ds((side * HEADS + n) * HD, HD)
                for g in range(3):
                    row = pl.multiple_of(g * HALF + core * QTR, QTR)
                    a_ref[pl.ds(row, QTR), col] = z_ref[src, core * HEADS + h, g]
                    row = pl.multiple_of(g * HALF + (1 - core) * QTR, QTR)
                    a_ref[pl.ds(row, QTR), col] = zo_ref[src, h, g]

    half = HEADS * HD
    acc = jnp.dot(a_ref[:, :half], w_ref[...], preferred_element_type=F32)
    acc += jnp.dot(a_ref[:, half : half + half // 2], wf_ref[...], preferred_element_type=F32)
    acc += jnp.dot(a_ref[:, half + half // 2 :], wr_ref[...], preferred_element_type=F32)
    o_ref[...] = acc.astype(BF)


def project(ids, z, zo, w, wf, wr):
    width = w.shape[1]
    half = HEADS * HD
    rows = 3 * HALF
    whole = lambda x: pl.BlockSpec(x.shape, lambda n: (0,) * x.ndim)
    return pl.pallas_call(
        project_kernel,
        grid=(width // COLS,),
        out_shape=jax.ShapeDtypeStruct((rows, width), BF),
        in_specs=[
            pl.BlockSpec(memory_space=pltpu.SMEM),
            whole(z),
            whole(zo),
            pl.BlockSpec((half, COLS), lambda n: (0, n)),
            pl.BlockSpec((half // 2, COLS), lambda n: (0, n)),
            pl.BlockSpec((half // 2, COLS), lambda n: (0, n)),
        ],
        out_specs=pl.BlockSpec((rows, COLS), lambda n: (0, n)),
        scratch_shapes=[pltpu.VMEM((rows, 2 * half), BF)],
        compiler_params=pltpu.CompilerParams(vmem_limit_bytes=48 << 20),
        name="project",
    )(ids, z, zo, w, wf, wr)


SWAP = [(0, 1), (1, 0)]


def shards(q, k, v, w, doc_lengths, spans, assignment):
    core = lax.axis_index("core").astype(jnp.int32)
    t_own = lax.axis_index("tensor").astype(jnp.int32)
    chip = lax.axis_index("context").astype(jnp.int32)

    depth = w.shape[0] // 2
    w_mine = lax.dynamic_slice_in_dim(w, core * depth, depth, 0)
    across = [(a * 2 + b, (1 - a) * 2 + 1 - b) for a in range(2) for b in range(2)]
    w_fetched = lax.ppermute(w_mine, ("z_lo", "tensor"), across)
    w_shared = lax.ppermute(w_fetched, "core", SWAP)

    ints = jnp.concatenate([doc_lengths, spans.reshape(-1), assignment])
    ints_other = lax.ppermute(ints, "core", SWAP)
    ints = jnp.where(chip // HEADS == core, ints, ints_other)
    ints = jnp.concatenate([core[None], ints])

    own, send = pack(core[None], q, k, v)
    recv = lax.ppermute(send, "core", SWAP)
    x = jnp.where(
        core == 0, jnp.concatenate([own, recv], axis=0), jnp.concatenate([recv, own], axis=0)
    )
    y = lax.all_to_all(x, "context", 0, 0, tiled=True).reshape(ROWS, 3 * HD)
    kvo = lax.ppermute(y[:, HD:], "core", SWAP)
    att = attend(ints, y, kvo)
    z = lax.all_to_all(
        att.reshape(2 * NCTX, 3, QTR, HD), ("tensor", "context"), 0, 0, tiled=True
    ).reshape(2, 2 * HEADS, 3, QTR, HD)
    z_send = lax.dynamic_slice_in_dim(z, (1 - core) * HEADS, HEADS, 1)
    zo = lax.ppermute(z_send, "core", SWAP)
    return project(jnp.stack([core, t_own]), z, zo, w, w_fetched, w_shared)


def solution(mesh):
    fine = Mesh(
        mesh.devices.reshape(2, 2, NCTX, 2), ("z_lo", "core", "context", "tensor")
    )
    dp = ("z_lo", "core")
    rows = P(dp + ("context",), "tensor")
    placed = (rows, rows, rows, P("tensor", None), P(dp), P(dp, None), P(dp))
    return jax.shard_map(
        shards,
        mesh=fine,
        in_specs=placed,
        out_specs=P(dp + ("context", "tensor"), None),
        check_vma=False,
    )
```

```python
import functools
import math

import jax
import jax.numpy as jnp
from jax import lax
from jax.experimental import pallas as pl
from jax.experimental.pallas import tpu as pltpu
from jax.sharding import Mesh, PartitionSpec as P

HD = 128
QB = 128
QTR = QB // 4
HALF = QB // 2
NCTX = 16
CHIP_BLOCKS = 3
NBLK = NCTX * CHIP_BLOCKS
HEADS = 8
ROWS = NBLK * HALF
NDOC = 6
NSPAN = 31
TILE = 4
TROWS = TILE * HALF
TPOS = TILE * QB
NTILE = NBLK // TILE
SCALE2 = math.log2(math.e) / math.sqrt(HD)
NEG = -1e30
BF = jnp.bfloat16
F32 = jnp.float32


def pack_kernel(core_ref, q_ref, k_ref, v_ref, own_ref, send_ref):
    core = core_ref[0]
    for out_ref, parity in ((own_ref, core), (send_ref, 1 - core)):
        for a, ref in enumerate((q_ref, k_ref, v_ref)):
            for group in range(2 * CHIP_BLOCKS):
                start = pl.multiple_of(group * HALF + parity * QTR, QTR)
                rows = ref[pl.ds(start, QTR), :]
                for h in range(HEADS):
                    out_ref[h, group * QTR : (group + 1) * QTR, a * HD : (a + 1) * HD] = rows[
                        :, h * HD : (h + 1) * HD
                    ]


def pack(core, q, k, v):
    out = jax.ShapeDtypeStruct((HEADS, CHIP_BLOCKS * HALF, 3 * HD), BF)
    vmem = pl.BlockSpec(memory_space=pltpu.VMEM)
    return pl.pallas_call(
        pack_kernel,
        out_shape=(out, out),
        in_specs=[pl.BlockSpec(memory_space=pltpu.SMEM), vmem, vmem, vmem],
        out_specs=(vmem, vmem),
        compiler_params=pltpu.CompilerParams(vmem_limit_bytes=32 << 20),
        name="pack",
    )(core, q, k, v)


def prepare_kernel(ints_ref, kdoc_ref, qdoc_ref, hi_ref, meta_ref):
    core = ints_ref[0]
    spans_at = 1 + NDOC
    assign_at = spans_at + 2 * NSPAN

    def half_pos(index, parity):
        return 2 * index - (index & (QTR - 1)) + parity * QTR

    lane = lax.broadcasted_iota(jnp.int32, (8, HD), 1)
    starts, start = [], jnp.int32(0)
    first = jnp.zeros((8, HD), jnp.int32)
    last = jnp.zeros((8, HD), jnp.int32)
    for d in range(NDOC):
        end = start + ints_ref[1 + d]
        first = jnp.where(lane == d, start, first)
        last = jnp.where(lane == d, end, last)
        starts.append(start)
        start = end
    first, last = first[:1], last[:1]
    used = lane[:1] < NDOC
    for c in range(NCTX):
        rows = slice(c * CHIP_BLOCKS * HALF, (c + 1) * CHIP_BLOCKS * HALF)
        index = lax.broadcasted_iota(jnp.int32, (CHIP_BLOCKS * HALF, HD), 0)
        base = half_pos(index, 0) + c * CHIP_BLOCKS * QB
        for n, parity in enumerate((core, 1 - core)):
            pos = base + parity * QTR
            inside = (pos >= first) & (pos < last)
            kdoc_ref[n, rows, :] = jnp.where(inside, 1.0, 0.0).astype(BF)
            if n == 0:
                qdoc_ref[rows, :] = jnp.where(inside | ~used, 0.0, NEG).astype(BF)

    def query_tile(j, c):
        tile_first = j * TPOS
        pos = half_pos(lax.broadcasted_iota(jnp.int32, (8, TROWS), 1), core) + tile_first

        def one_span(s, hi):
            a = ints_ref[spans_at + 2 * s]
            b = ints_ref[spans_at + 2 * s + 1]
            return jnp.where((pos >= a) & (pos < b), b, hi)

        hi = lax.fori_loop(0, NSPAN, one_span, pos + 1, unroll=True)
        hi_ref[j] = hi - tile_first
        lo_first = jnp.int32(0)
        for d in range(NDOC):
            lo_first = jnp.where(tile_first >= starts[d], starts[d], lo_first)
        before = j - lo_first // TPOS
        after = jnp.where(jnp.max(hi) > tile_first + TPOS, 1, 0)
        after = jnp.where(j == NTILE - 1, 0, after)
        meta_ref[j] = 2 * before + after
        return c

    lax.fori_loop(0, NTILE, query_tile, 0)

    def invert(j, c):
        meta_ref[NTILE + ints_ref[assign_at + j]] = j
        return c

    lax.fori_loop(0, NBLK, invert, 0)


def prepare(ints):
    vmem = pl.BlockSpec(memory_space=pltpu.VMEM)
    smem = pl.BlockSpec(memory_space=pltpu.SMEM)
    return pl.pallas_call(
        prepare_kernel,
        out_shape=(
            jax.ShapeDtypeStruct((2, ROWS, HD), BF),
            jax.ShapeDtypeStruct((ROWS, HD), BF),
            jax.ShapeDtypeStruct((NTILE, 8, TROWS), jnp.int32),
            jax.ShapeDtypeStruct((NTILE + NBLK,), jnp.int32),
        ),
        in_specs=[smem],
        out_specs=(vmem, vmem, vmem, smem),
        compiler_params=pltpu.CompilerParams(vmem_limit_bytes=32 << 20),
        name="prepare",
    )(ints)


AHEAD = 2 * HALF
MAXBEFORE = 3


def attend_kernel(core_ref, meta_ref, y_ref, kvo_ref, kdoc_ref, qdoc_ref, hi_ref, o_ref):
    core = core_ref[0]

    def half_pos(index):
        return 2 * index - (index & (QTR - 1))

    def query_tile(j, c):
        qrows = pl.ds(pl.multiple_of(j * TROWS, TROWS), TROWS)
        q = jnp.concatenate([y_ref[qrows, :HD], qdoc_ref[qrows, :]], axis=1)

        def run(before, after):
            start = pl.multiple_of((j - before) * TROWS, TROWS)
            count = (before + 1) * TROWS + after * AHEAD
            rows = pl.ds(start, count)
            own = (y_ref[rows, HD : 2 * HD], y_ref[rows, 2 * HD :], kdoc_ref[0, rows, :], core)
            other = (kvo_ref[rows, :HD], kvo_ref[rows, HD:], kdoc_ref[1, rows, :], 1 - core)
            scores = []
            tail = before * TROWS
            key_pos = half_pos(lax.broadcasted_iota(jnp.int32, (count - tail, TROWS), 0))
            for key, _, doc, parity in (own, other):
                s = lax.dot_general(
                    jnp.concatenate([key, doc], axis=1),
                    q,
                    (((1,), (1,)), ((), ())),
                    preferred_element_type=F32,
                )
                end = jnp.where(key_pos < hi_ref[j, :1, :] - parity * QTR, s[tail:], NEG)
                scores.append([s[:tail], end] if before else [end])
            peak = functools.reduce(
                jnp.maximum, [jnp.max(s, axis=0, keepdims=True) for part in scores for s in part]
            )
            l = jnp.zeros((1, TROWS), F32)
            acc = jnp.zeros((HD, TROWS), F32)
            for part, (_, value, _, _) in zip(scores, (own, other)):
                weights = []
                for s in part:
                    p = jnp.exp2((s - peak) * SCALE2)
                    l = l + jnp.sum(p, axis=0, keepdims=True)
                    weights.append(p.astype(BF))
                p = jnp.concatenate(weights, axis=0) if before else weights[0]
                acc = acc + lax.dot_general(
                    value, p, (((0,), (0,)), ((), ())), preferred_element_type=F32
                )
            out = jnp.transpose(acc / l).astype(BF)
            for b in range(TILE):
                slot = meta_ref[NTILE + j * TILE + b]
                chip = slot // CHIP_BLOCKS
                for u in range(2):
                    group = (slot % CHIP_BLOCKS) * 2 + u
                    o_ref[group // 3, chip, group % 3] = out[
                        b * HALF + u * QTR : b * HALF + (u + 1) * QTR
                    ]

        case = meta_ref[j]
        for before in range(MAXBEFORE + 1):
            for after in range(2):
                pl.when(case == 2 * before + after)(functools.partial(run, before, after))
        return c

    lax.fori_loop(0, NTILE, query_tile, 0)


def attend(core, meta, y, kvo, kdoc, qdoc, hi):
    vmem = pl.BlockSpec(memory_space=pltpu.VMEM)
    smem = pl.BlockSpec(memory_space=pltpu.SMEM)
    return pl.pallas_call(
        attend_kernel,
        out_shape=jax.ShapeDtypeStruct((2, NCTX, 3, QTR, HD), BF),
        in_specs=[smem, smem] + [vmem] * 5,
        out_specs=vmem,
        compiler_params=pltpu.CompilerParams(vmem_limit_bytes=40 << 20),
        name="attend",
    )(core, meta, y, kvo, kdoc, qdoc, hi)


COLS = 512
CTX = ("y", "x")
NLINE = 4
CHUNKS = 1
PIECE = HEADS * HD // NLINE // CHUNKS
PHEADS = PIECE // HD


def project_kernel(ids_ref, z_ref, zo_ref, w_ref, *refs):
    count = (len(refs) - 3) // 2
    weights, (o_ref, a_ref, b_ref) = (refs[:count], refs[count : 2 * count]), refs[2 * count :]
    core, t_own = ids_ref[0], ids_ref[1]
    step = pl.program_id(0)

    @pl.when(step == 0)
    def _():
        def head(ref, at, src, h):
            col = slice(at * HD, (at + 1) * HD)
            for g in range(3):
                row = pl.multiple_of(g * HALF + core * QTR, QTR)
                ref[pl.ds(row, QTR), col] = z_ref[src, core * HEADS + h, g]
                row = pl.multiple_of(g * HALF + (1 - core) * QTR, QTR)
                ref[pl.ds(row, QTR), col] = zo_ref[src, h, g]

        for h in range(HEADS):
            head(a_ref, h, t_own, h)
        for half in range(2):
            for n in range(CHUNKS * NLINE):
                piece = (n & -NLINE) + ((ids_ref[2 + half] + n) & (NLINE - 1))
                for h in range(PHEADS):
                    head(b_ref.at[half], n * PHEADS + h, 1 - t_own, piece * PHEADS + h)

    own = HEADS * HD

    def run(half):
        acc = jnp.dot(a_ref[:, :own], w_ref[...], preferred_element_type=F32)
        at = 0
        for ref in weights[half]:
            depth = ref.shape[0]
            acc += jnp.dot(
                b_ref[half, :, at : at + depth], ref[...], preferred_element_type=F32
            )
            at += depth
        o_ref[...] = acc.astype(BF)

    steps = pl.num_programs(0) // 2
    pl.when(step < steps)(functools.partial(run, 0))
    pl.when(step >= steps)(functools.partial(run, 1))


def project(ids, z, zo, w, mine, other):
    width = w.shape[1]
    rows = 3 * HALF
    steps = width // COLS // 2
    whole = lambda x: pl.BlockSpec(x.shape, lambda n, ids: (0,) * x.ndim)
    column = lambda n, ids: (0, (n + ids[0] * steps) & (2 * steps - 1))
    first = lambda n, ids: (0, jnp.minimum(n, steps - 1))
    second = lambda n, ids: (0, jnp.maximum(n - steps, 0))
    return pl.pallas_call(
        project_kernel,
        grid_spec=pltpu.PrefetchScalarGridSpec(
            num_scalar_prefetch=1,
            grid=(2 * steps,),
            in_specs=[whole(z), whole(zo), pl.BlockSpec((HEADS * HD, COLS), column)]
            + [pl.BlockSpec((m.shape[0], COLS), first) for m in mine]
            + [pl.BlockSpec((m.shape[0], COLS), second) for m in other],
            out_specs=pl.BlockSpec((rows, COLS), column),
            scratch_shapes=[
                pltpu.VMEM((rows, HEADS * HD), BF),
                pltpu.VMEM((2, rows, HEADS * HD), BF),
            ],
        ),
        out_shape=jax.ShapeDtypeStruct((rows, width), BF),
        compiler_params=pltpu.CompilerParams(vmem_limit_bytes=48 << 20),
        name="project",
    )(ids, z, zo, w, *mine, *other)


SWAP = [(0, 1), (1, 0)]


def swap(x):
    return lax.ppermute(x, "core", SWAP)


def after(values, *others):
    return lax.optimization_barrier((values,) + others)[0]


def along_line(x, step):
    pairs = []
    for y in range(NLINE):
        for x_at in range(NLINE):
            for core in range(2):
                to = (y, (x_at - step) % NLINE) if core == 0 else ((y - step) % NLINE, x_at)
                index = lambda y, x: (core * NLINE + y) * NLINE + x
                pairs.append((index(y, x_at), index(*to)))
    return lax.ppermute(x, ("core",) + CTX, pairs)


def shards(q, k, v, w, doc_lengths, spans, assignment):
    core = lax.axis_index("core").astype(jnp.int32)
    t_own = lax.axis_index("tensor").astype(jnp.int32)
    x_at = lax.axis_index("x").astype(jnp.int32)
    y_at = lax.axis_index("y").astype(jnp.int32)
    chip = y_at * NLINE + x_at

    across = [(a * 2 + b, (1 - a) * 2 + 1 - b) for a in range(2) for b in range(2)]
    from_z = lambda x: lax.ppermute(x, ("z_lo", "tensor"), across)
    half = w.shape[1] // 2
    line = jnp.where(core == 0, x_at, y_at)
    fetched = [
        from_z(lax.dynamic_slice(w, (PIECE * (c * NLINE + line), core * half), (PIECE, half)))
        for c in range(CHUNKS)
    ]

    ints = jnp.concatenate([doc_lengths, spans.reshape(-1), assignment])
    ints = jnp.where(chip // HEADS == core, ints, swap(ints))
    ints = jnp.concatenate([core[None], ints])

    own, send = pack(core[None], q, k, v)
    recv = swap(send)
    x = jnp.where(
        core == 0, jnp.concatenate([own, recv], axis=0), jnp.concatenate([recv, own], axis=0)
    )
    y = lax.all_to_all(x, CTX, 0, 0, tiled=True).reshape(ROWS, 3 * HD)
    kdoc, qdoc, hi, meta = prepare(ints)
    y, kdoc, qdoc, hi, meta = lax.optimization_barrier((y, kdoc, qdoc, hi, meta))
    y, fetched = lax.optimization_barrier((y, fetched))
    kvo = swap(y[:, HD:])

    pieces = [[piece] + [along_line(piece, step) for step in (1, 2, 3)] for piece in fetched]
    att = attend(core[None], meta, y, kvo, kdoc, qdoc, hi)
    att, pieces = lax.optimization_barrier((att, pieces))
    mine = sum(pieces, [])
    other = [swap(p) for p in mine]
    z = lax.all_to_all(
        att.reshape(2 * NCTX, 3, QTR, HD), ("tensor",) + CTX, 0, 0, tiled=True
    ).reshape(2, 2 * HEADS, 3, QTR, HD)
    zo = swap(lax.dynamic_slice_in_dim(z, (1 - core) * HEADS, HEADS, 1))
    lines = jnp.where(core == 0, jnp.stack([x_at, y_at]), jnp.stack([y_at, x_at]))
    ids = jnp.concatenate([jnp.stack([core, t_own]), lines])
    return project(ids, z, zo, w, mine, other)


def solution(mesh):
    fine = Mesh(
        mesh.devices.reshape(2, 2, NLINE, NLINE, 2), ("z_lo", "core", "y", "x", "tensor")
    )
    dp = ("z_lo", "core")
    rows = P(dp + CTX, "tensor")
    placed = (rows, rows, rows, P("tensor", None), P(dp), P(dp, None), P(dp))
    return jax.shard_map(
        shards,
        mesh=fine,
        in_specs=placed,
        out_specs=P(dp + CTX + ("tensor",), None),
        check_vma=False,
    )
```

```python
import functools
import math

import jax
import jax.numpy as jnp
from jax import lax
from jax.experimental import pallas as pl
from jax.experimental.pallas import tpu as pltpu
from jax.sharding import Mesh, PartitionSpec as P

HD = 128
QB = 128
QTR = QB // 4
HALF = QB // 2
NCTX = 16
CHIP_BLOCKS = 3
NBLK = NCTX * CHIP_BLOCKS
HEADS = 8
ROWS = NBLK * HALF
NDOC = 6
NSPAN = 31
TILE = 4
TROWS = TILE * HALF
TPOS = TILE * QB
NTILE = NBLK // TILE
SCALE2 = math.log2(math.e) / math.sqrt(HD)
NEG = -1e30
BF = jnp.bfloat16
F32 = jnp.float32


def pack_kernel(core_ref, q_hbm, k_hbm, v_hbm, own_ref, send_ref, buf, sems):
    core = core_ref[0]
    copies = []
    for block in range(CHIP_BLOCKS):
        rows = slice(block * QB, (block + 1) * QB)
        for a, ref in enumerate((q_hbm, k_hbm, v_hbm)):
            copy = pltpu.make_async_copy(ref.at[rows], buf.at[a, rows], sems.at[block, a])
            copy.start()
            copies.append(copy)
    for block in range(CHIP_BLOCKS):
        for a in range(3):
            copies[block * 3 + a].wait()
            for out_ref, parity in ((own_ref, core), (send_ref, 1 - core)):
                for group in (2 * block, 2 * block + 1):
                    start = pl.multiple_of(group * HALF + parity * QTR, QTR)
                    rows = buf[a, pl.ds(start, QTR), :]
                    for h in range(HEADS):
                        out_ref[
                            h, group * QTR : (group + 1) * QTR, a * HD : (a + 1) * HD
                        ] = rows[:, h * HD : (h + 1) * HD]


def pack(core, q, k, v):
    out = jax.ShapeDtypeStruct((HEADS, CHIP_BLOCKS * HALF, 3 * HD), BF)
    vmem = pl.BlockSpec(memory_space=pltpu.VMEM)
    hbm = pl.BlockSpec(memory_space=pltpu.HBM)
    return pl.pallas_call(
        pack_kernel,
        out_shape=(out, out),
        in_specs=[pl.BlockSpec(memory_space=pltpu.SMEM), hbm, hbm, hbm],
        out_specs=(vmem, vmem),
        scratch_shapes=[
            pltpu.VMEM((3,) + q.shape, BF),
            pltpu.SemaphoreType.DMA((CHIP_BLOCKS, 3)),
        ],
        compiler_params=pltpu.CompilerParams(vmem_limit_bytes=12 << 20),
        name="pack",
    )(core, q, k, v)


def merge_kernel(core_ref, own_ref, recv_ref, o_ref):
    core = core_ref[0]
    o_ref[pl.ds(core * HEADS, HEADS)] = own_ref[...]
    o_ref[pl.ds((1 - core) * HEADS, HEADS)] = recv_ref[...]


def merge(core, own, recv):
    vmem = pl.BlockSpec(memory_space=pltpu.VMEM)
    return pl.pallas_call(
        merge_kernel,
        out_shape=jax.ShapeDtypeStruct((2 * HEADS,) + own.shape[1:], BF),
        in_specs=[pl.BlockSpec(memory_space=pltpu.SMEM), vmem, vmem],
        out_specs=vmem,
        compiler_params=pltpu.CompilerParams(vmem_limit_bytes=12 << 20),
        name="merge",
    )(core, own, recv)


def prepare_kernel(ints_ref, kdoc_ref, qdoc_ref, hi_ref, meta_ref):
    core = ints_ref[0]
    spans_at = 1 + NDOC
    assign_at = spans_at + 2 * NSPAN

    def half_pos(index, parity):
        return 2 * index - (index & (QTR - 1)) + parity * QTR

    lane = lax.broadcasted_iota(jnp.int32, (8, HD), 1)
    starts, start = [], jnp.int32(0)
    first = jnp.zeros((8, HD), jnp.int32)
    last = jnp.zeros((8, HD), jnp.int32)
    for d in range(NDOC):
        end = start + ints_ref[1 + d]
        first = jnp.where(lane == d, start, first)
        last = jnp.where(lane == d, end, last)
        starts.append(start)
        start = end
    first, last = first[:1], last[:1]
    used = lane[:1] < NDOC
    for c in range(NCTX):
        rows = slice(c * CHIP_BLOCKS * HALF, (c + 1) * CHIP_BLOCKS * HALF)
        index = lax.broadcasted_iota(jnp.int32, (CHIP_BLOCKS * HALF, HD), 0)
        base = half_pos(index, 0) + c * CHIP_BLOCKS * QB
        for n, parity in enumerate((core, 1 - core)):
            pos = base + parity * QTR
            inside = (pos >= first) & (pos < last)
            kdoc_ref[n, rows, :] = jnp.where(inside, 1.0, 0.0).astype(BF)
            if n == 0:
                qdoc_ref[rows, :] = jnp.where(inside | ~used, 0.0, NEG).astype(BF)

    def query_tile(j, c):
        tile_first = j * TPOS
        pos = half_pos(lax.broadcasted_iota(jnp.int32, (8, TROWS), 1), core) + tile_first

        def one_span(s, hi):
            a = ints_ref[spans_at + 2 * s]
            b = ints_ref[spans_at + 2 * s + 1]
            return jnp.where((pos >= a) & (pos < b), b, hi)

        hi = lax.fori_loop(0, NSPAN, one_span, pos + 1, unroll=True)
        hi_ref[j] = hi - tile_first
        lo_first = jnp.int32(0)
        for d in range(NDOC):
            lo_first = jnp.where(tile_first >= starts[d], starts[d], lo_first)
        before = j - lo_first // TPOS
        after = jnp.where(jnp.max(hi) > tile_first + TPOS, 1, 0)
        after = jnp.where(j == NTILE - 1, 0, after)
        meta_ref[j] = 2 * before + after
        return c

    lax.fori_loop(0, NTILE, query_tile, 0)

    def invert(j, c):
        meta_ref[NTILE + ints_ref[assign_at + j]] = j
        return c

    lax.fori_loop(0, NBLK, invert, 0)


def prepare(ints):
    vmem = pl.BlockSpec(memory_space=pltpu.VMEM)
    smem = pl.BlockSpec(memory_space=pltpu.SMEM)
    return pl.pallas_call(
        prepare_kernel,
        out_shape=(
            jax.ShapeDtypeStruct((2, ROWS, HD), BF),
            jax.ShapeDtypeStruct((ROWS, HD), BF),
            jax.ShapeDtypeStruct((NTILE, 8, TROWS), jnp.int32),
            jax.ShapeDtypeStruct((NTILE + NBLK,), jnp.int32),
        ),
        in_specs=[smem],
        out_specs=(vmem, vmem, vmem, smem),
        compiler_params=pltpu.CompilerParams(vmem_limit_bytes=12 << 20),
        name="prepare",
    )(ints)


AHEAD = 2 * HALF
MAXBEFORE = 3


def attend_kernel(core_ref, meta_ref, y_ref, kvo_ref, kdoc_ref, qdoc_ref, hi_ref, o_ref):
    core = core_ref[0]

    def half_pos(index):
        return 2 * index - (index & (QTR - 1))

    def query_tile(j, c):
        qrows = pl.ds(pl.multiple_of(j * TROWS, TROWS), TROWS)
        q = jnp.concatenate([y_ref[qrows, :HD], qdoc_ref[qrows, :]], axis=1)

        def run(before, after):
            start = pl.multiple_of((j - before) * TROWS, TROWS)
            count = (before + 1) * TROWS + after * AHEAD
            rows = pl.ds(start, count)
            own = (y_ref[rows, HD : 2 * HD], y_ref[rows, 2 * HD :], kdoc_ref[0, rows, :], core)
            other = (kvo_ref[rows, :HD], kvo_ref[rows, HD:], kdoc_ref[1, rows, :], 1 - core)
            scores = []
            tail = before * TROWS
            key_pos = half_pos(lax.broadcasted_iota(jnp.int32, (count - tail, TROWS), 0))
            for key, _, doc, parity in (own, other):
                s = lax.dot_general(
                    jnp.concatenate([key, doc], axis=1),
                    q,
                    (((1,), (1,)), ((), ())),
                    preferred_element_type=F32,
                )
                end = jnp.where(key_pos < hi_ref[j, :1, :] - parity * QTR, s[tail:], NEG)
                scores.append([s[:tail], end] if before else [end])
            peak = functools.reduce(
                jnp.maximum, [jnp.max(s, axis=0, keepdims=True) for part in scores for s in part]
            )
            l = jnp.zeros((1, TROWS), F32)
            acc = jnp.zeros((HD, TROWS), F32)
            for part, (_, value, _, _) in zip(scores, (own, other)):
                weights = []
                for s in part:
                    p = jnp.exp2((s - peak) * SCALE2)
                    l = l + jnp.sum(p, axis=0, keepdims=True)
                    weights.append(p.astype(BF))
                p = jnp.concatenate(weights, axis=0) if before else weights[0]
                acc = acc + lax.dot_general(
                    value, p, (((0,), (0,)), ((), ())), preferred_element_type=F32
                )
            out = jnp.transpose(acc / l).astype(BF)
            for b in range(TILE):
                slot = meta_ref[NTILE + j * TILE + b]
                chip = slot // CHIP_BLOCKS
                for u in range(2):
                    group = (slot % CHIP_BLOCKS) * 2 + u
                    o_ref[group // 3, chip, group % 3] = out[
                        b * HALF + u * QTR : b * HALF + (u + 1) * QTR
                    ]

        case = meta_ref[j]
        for before in range(MAXBEFORE + 1):
            for after in range(2):
                pl.when(case == 2 * before + after)(functools.partial(run, before, after))
        return c

    lax.fori_loop(0, NTILE, query_tile, 0)


def attend(core, meta, y, kvo, kdoc, qdoc, hi):
    vmem = pl.BlockSpec(memory_space=pltpu.VMEM)
    smem = pl.BlockSpec(memory_space=pltpu.SMEM)
    return pl.pallas_call(
        attend_kernel,
        out_shape=jax.ShapeDtypeStruct((2, NCTX, 3, QTR, HD), BF),
        in_specs=[smem, smem] + [vmem] * 5,
        out_specs=vmem,
        compiler_params=pltpu.CompilerParams(vmem_limit_bytes=14 << 20),
        name="attend",
    )(core, meta, y, kvo, kdoc, qdoc, hi)


SHARED = 1536
LOADS = 8
DIRECT = (256, 256)
CTX = ("y", "x")
NLINE = 4
PIECE = HEADS * HD // NLINE
PHEADS = PIECE // HD


def project_kernel(ids_ref, z_ref, zo_ref, w_ref, *refs):
    count = NLINE + len(DIRECT)
    sides = (refs[:count], refs[count : 2 * count])
    o_ref, a_ref, b_ref = refs[2 * count : 2 * count + 3]
    bufs, (acc_ref, w_buf, sems) = refs[2 * count + 3 : -3], refs[-3:]
    core, t_own = ids_ref[0], ids_ref[1]
    half = w_ref.shape[1] // 2

    loads = []
    rows = w_ref.shape[0] // LOADS
    for n in range(LOADS):
        part = slice(n * rows, (n + 1) * rows)
        loads.append(pltpu.make_async_copy(w_ref.at[part], w_buf.at[part], sems.at[2, n]))
        loads[-1].start()

    steps = []
    for side in range(2):
        first = (core if side == 0 else 1 - core) * half
        start = 0
        for n, width in enumerate((SHARED,) + DIRECT):
            column = pl.ds(pl.multiple_of(first + start, HD), width)
            steps.append((side, n, column, slice(side * half + start, side * half + start + width)))
            start += width

    def head(ref, at, src, h):
        col = slice(at * HD, (at + 1) * HD)
        for g in range(3):
            row = pl.multiple_of(g * HALF + core * QTR, QTR)
            ref[pl.ds(row, QTR), col] = z_ref[src, core * HEADS + h, g]
            row = pl.multiple_of(g * HALF + (1 - core) * QTR, QTR)
            ref[pl.ds(row, QTR), col] = zo_ref[src, h, g]

    for h in range(HEADS):
        head(a_ref, h, t_own, h)
        head(b_ref.at[2], h, 1 - t_own, h)
    for side in range(2):
        for n in range(NLINE):
            piece = (ids_ref[2 + side] + n) & (NLINE - 1)
            for h in range(PHEADS):
                head(b_ref.at[side], n * PHEADS + h, 1 - t_own, piece * PHEADS + h)

    for side, n, _, place in steps:
        if n == 0:
            acc = 0.0
            for m in range(NLINE):
                acc += jnp.dot(
                    b_ref[side, :, m * PIECE : (m + 1) * PIECE],
                    sides[side][m][...],
                    preferred_element_type=F32,
                )
        else:
            acc = jnp.dot(b_ref[2], sides[side][NLINE + n - 1][...], preferred_element_type=F32)
        acc_ref[:, place] = acc
    for copy in loads:
        copy.wait()
    stores = []
    for side, n, column, place in steps:
        acc = acc_ref[:, place] + jnp.dot(
            a_ref[...], w_buf[:, column], preferred_element_type=F32
        )
        buf = bufs[n].at[side]
        buf[...] = acc.astype(BF)
        store = pltpu.make_async_copy(buf, o_ref.at[:, column], sems.at[side, n])
        store.start()
        stores.append(store)
    for store in stores:
        store.wait()


def project(ids, z, zo, w, mine, other):
    width = w.shape[1]
    depth = HEADS * HD
    rows = 3 * HALF
    parts = mine + other
    widths = (SHARED,) + DIRECT
    vmem = pl.BlockSpec(memory_space=pltpu.VMEM)
    hbm = pl.BlockSpec(memory_space=pltpu.HBM)
    return pl.pallas_call(
        project_kernel,
        in_specs=[pl.BlockSpec(memory_space=pltpu.SMEM), vmem, vmem, hbm] + [vmem] * len(parts),
        out_specs=hbm,
        out_shape=jax.ShapeDtypeStruct((rows, width), BF),
        scratch_shapes=[pltpu.VMEM((rows, depth), BF), pltpu.VMEM((3, rows, depth), BF)]
        + [pltpu.VMEM((2, rows, n), BF) for n in widths]
        + [
            pltpu.VMEM((rows, width), F32),
            pltpu.VMEM((depth, width), BF),
            pltpu.SemaphoreType.DMA((3, LOADS)),
        ],
        compiler_params=pltpu.CompilerParams(vmem_limit_bytes=24 << 20),
        name="project",
    )(ids, z, zo, w, *parts)


def pick_kernel(core_ref, z_ref, o_ref):
    o_ref[...] = z_ref[:, pl.ds((1 - core_ref[0]) * HEADS, HEADS)]


def pick(core, z):
    vmem = pl.BlockSpec(memory_space=pltpu.VMEM)
    return pl.pallas_call(
        pick_kernel,
        out_shape=jax.ShapeDtypeStruct((2, HEADS) + z.shape[2:], BF),
        in_specs=[pl.BlockSpec(memory_space=pltpu.SMEM), vmem],
        out_specs=vmem,
        compiler_params=pltpu.CompilerParams(vmem_limit_bytes=4 << 20),
        name="pick",
    )(core, z)


SWAP = [(0, 1), (1, 0)]


def swap(x):
    return lax.ppermute(x, "core", SWAP)


def in_vmem(x):
    return pltpu.with_memory_space_constraint(x, pltpu.VMEM)


def after(values, *others):
    return lax.optimization_barrier((values,) + others)[0]


def along_line(x, step):
    pairs = []
    for y in range(NLINE):
        for x_at in range(NLINE):
            for core in range(2):
                to = (y, (x_at - step) % NLINE) if core == 0 else ((y - step) % NLINE, x_at)
                index = lambda y, x: (core * NLINE + y) * NLINE + x
                pairs.append((index(y, x_at), index(*to)))
    return lax.ppermute(x, ("core",) + CTX, pairs)


def shards(q, k, v, w, doc_lengths, spans, assignment):
    core = lax.axis_index("core").astype(jnp.int32)
    t_own = lax.axis_index("tensor").astype(jnp.int32)
    x_at = lax.axis_index("x").astype(jnp.int32)
    y_at = lax.axis_index("y").astype(jnp.int32)
    chip = y_at * NLINE + x_at

    across = [(a * 2 + b, (1 - a) * 2 + 1 - b) for a in range(2) for b in range(2)]
    from_z = lambda x: lax.ppermute(x, ("z_lo", "tensor"), across)
    half = w.shape[1] // 2
    line = jnp.where(core == 0, x_at, y_at)
    piece = from_z(lax.dynamic_slice(w, (PIECE * line, core * half), (PIECE, SHARED)))
    direct, at = [], core * half + SHARED
    for width in DIRECT:
        direct.append(lax.dynamic_slice(w, (0, at), (w.shape[0], width)))
        at += width
    first = from_z(after(direct[0], piece))

    ints = jnp.concatenate([doc_lengths, spans.reshape(-1), assignment])
    ints = jnp.where(chip // HEADS == core, ints, swap(ints))
    ints = jnp.concatenate([core[None], ints])

    q, k, v = (pltpu.with_memory_space_constraint(x, pltpu.HBM) for x in (q, k, v))
    own, send = pack(core[None], q, k, v)
    recv = swap(send)
    x = merge(core[None], own, recv)
    y = lax.all_to_all(x, CTX, 0, 0, tiled=True).reshape(ROWS, 3 * HD)
    kdoc, qdoc, hi, meta = prepare(ints)
    y, kdoc, qdoc, hi, meta = lax.optimization_barrier((y, kdoc, qdoc, hi, meta))
    y, piece, first = lax.optimization_barrier((y, piece, first))
    second = from_z(after(direct[1], first))
    kvo = swap(y[:, HD:])

    pieces = [piece] + [along_line(piece, step) for step in (1, 2, 3)]
    att = attend(core[None], meta, y, kvo, kdoc, qdoc, hi)
    att, mine = lax.optimization_barrier((att, pieces + [first, second]))
    other = [swap(p) for p in mine]
    z = lax.all_to_all(
        att.reshape(2 * NCTX, 3, QTR, HD), ("tensor",) + CTX, 0, 0, tiled=True
    ).reshape(2, 2 * HEADS, 3, QTR, HD)
    zo = swap(pick(core[None], z))
    lines = jnp.where(core == 0, jnp.stack([x_at, y_at]), jnp.stack([y_at, x_at]))
    ids = jnp.concatenate([jnp.stack([core, t_own]), lines])
    mine, other = ([in_vmem(p) for p in side] for side in (mine, other))
    return project(ids, z, zo, pltpu.with_memory_space_constraint(w, pltpu.HBM), mine, other)


def solution(mesh):
    fine = Mesh(
        mesh.devices.reshape(2, 2, NLINE, NLINE, 2), ("z_lo", "core", "y", "x", "tensor")
    )
    dp = ("z_lo", "core")
    rows = P(dp + CTX, "tensor")
    placed = (rows, rows, rows, P("tensor", None), P(dp), P(dp, None), P(dp))
    return jax.shard_map(
        shards,
        mesh=fine,
        in_specs=placed,
        out_specs=P(dp + CTX + ("tensor",), None),
        check_vma=False,
    )
```

```python
import functools
import math

import jax
import jax.numpy as jnp
from jax import lax
from jax.experimental import pallas as pl
from jax.experimental.pallas import tpu as pltpu
from jax.sharding import Mesh, PartitionSpec as P

HD = 128
QB = 128
QTR = QB // 4
HALF = QB // 2
NCTX = 16
CHIP_BLOCKS = 3
NBLK = NCTX * CHIP_BLOCKS
HEADS = 8
ROWS = NBLK * HALF
NDOC = 6
NSPAN = 31
TILE = 4
TROWS = TILE * HALF
TPOS = TILE * QB
NTILE = NBLK // TILE
SCALE2 = math.log2(math.e) / math.sqrt(HD)
NEG = -1e30
BF = jnp.bfloat16
F32 = jnp.float32


def pack_kernel(core_ref, q_hbm, k_hbm, v_hbm, own_ref, send_ref, buf, sems):
    core = core_ref[0]
    copies = []
    for block in range(CHIP_BLOCKS):
        rows = slice(block * QB, (block + 1) * QB)
        for a, ref in enumerate((q_hbm, k_hbm, v_hbm)):
            copy = pltpu.make_async_copy(ref.at[rows], buf.at[a, rows], sems.at[block, a])
            copy.start()
            copies.append(copy)
    for block in range(CHIP_BLOCKS):
        for a in range(3):
            copies[block * 3 + a].wait()
            for out_ref, parity in ((own_ref, core), (send_ref, 1 - core)):
                for group in (2 * block, 2 * block + 1):
                    start = pl.multiple_of(group * HALF + parity * QTR, QTR)
                    rows = buf[a, pl.ds(start, QTR), :]
                    for h in range(HEADS):
                        out_ref[
                            h, group * QTR : (group + 1) * QTR, a * HD : (a + 1) * HD
                        ] = rows[:, h * HD : (h + 1) * HD]


def pack(core, q, k, v):
    out = jax.ShapeDtypeStruct((HEADS, CHIP_BLOCKS * HALF, 3 * HD), BF)
    vmem = pl.BlockSpec(memory_space=pltpu.VMEM)
    hbm = pl.BlockSpec(memory_space=pltpu.HBM)
    return pl.pallas_call(
        pack_kernel,
        out_shape=(out, out),
        in_specs=[pl.BlockSpec(memory_space=pltpu.SMEM), hbm, hbm, hbm],
        out_specs=(vmem, vmem),
        scratch_shapes=[
            pltpu.VMEM((3,) + q.shape, BF),
            pltpu.SemaphoreType.DMA((CHIP_BLOCKS, 3)),
        ],
        compiler_params=pltpu.CompilerParams(vmem_limit_bytes=12 << 20),
        name="pack",
    )(core, q, k, v)


def merge_kernel(core_ref, own_ref, recv_ref, o_ref):
    core = core_ref[0]
    o_ref[pl.ds(core * HEADS, HEADS)] = own_ref[...]
    o_ref[pl.ds((1 - core) * HEADS, HEADS)] = recv_ref[...]


def merge(core, own, recv):
    vmem = pl.BlockSpec(memory_space=pltpu.VMEM)
    return pl.pallas_call(
        merge_kernel,
        out_shape=jax.ShapeDtypeStruct((2 * HEADS,) + own.shape[1:], BF),
        in_specs=[pl.BlockSpec(memory_space=pltpu.SMEM), vmem, vmem],
        out_specs=vmem,
        compiler_params=pltpu.CompilerParams(vmem_limit_bytes=12 << 20),
        name="merge",
    )(core, own, recv)


def prepare_kernel(ints_ref, kdoc_ref, qdoc_ref, hi_ref, meta_ref):
    core = ints_ref[0]
    spans_at = 1 + NDOC
    assign_at = spans_at + 2 * NSPAN

    def half_pos(index, parity):
        return 2 * index - (index & (QTR - 1)) + parity * QTR

    lane = lax.broadcasted_iota(jnp.int32, (8, HD), 1)
    starts, start = [], jnp.int32(0)
    first = jnp.zeros((8, HD), jnp.int32)
    last = jnp.zeros((8, HD), jnp.int32)
    for d in range(NDOC):
        end = start + ints_ref[1 + d]
        first = jnp.where(lane == d, start, first)
        last = jnp.where(lane == d, end, last)
        starts.append(start)
        start = end
    first, last = first[:1], last[:1]
    used = lane[:1] < NDOC
    for c in range(NCTX):
        rows = slice(c * CHIP_BLOCKS * HALF, (c + 1) * CHIP_BLOCKS * HALF)
        index = lax.broadcasted_iota(jnp.int32, (CHIP_BLOCKS * HALF, HD), 0)
        base = half_pos(index, 0) + c * CHIP_BLOCKS * QB
        for n, parity in enumerate((core, 1 - core)):
            pos = base + parity * QTR
            inside = (pos >= first) & (pos < last)
            kdoc_ref[n, rows, :] = jnp.where(inside, 1.0, 0.0).astype(BF)
            if n == 0:
                qdoc_ref[rows, :] = jnp.where(inside | ~used, 0.0, NEG).astype(BF)

    def query_tile(j, c):
        tile_first = j * TPOS
        pos = half_pos(lax.broadcasted_iota(jnp.int32, (8, TROWS), 1), core) + tile_first

        def one_span(s, hi):
            a = ints_ref[spans_at + 2 * s]
            b = ints_ref[spans_at + 2 * s + 1]
            return jnp.where((pos >= a) & (pos < b), b, hi)

        hi = lax.fori_loop(0, NSPAN, one_span, pos + 1, unroll=True)
        hi_ref[j] = hi - tile_first
        lo_first = jnp.int32(0)
        for d in range(NDOC):
            lo_first = jnp.where(tile_first >= starts[d], starts[d], lo_first)
        before = j - lo_first // TPOS
        after = jnp.where(jnp.max(hi) > tile_first + TPOS, 1, 0)
        after = jnp.where(j == NTILE - 1, 0, after)
        meta_ref[j] = 2 * before + after
        return c

    lax.fori_loop(0, NTILE, query_tile, 0)

    def invert(j, c):
        meta_ref[NTILE + ints_ref[assign_at + j]] = j
        return c

    lax.fori_loop(0, NBLK, invert, 0)


def prepare(ints):
    vmem = pl.BlockSpec(memory_space=pltpu.VMEM)
    smem = pl.BlockSpec(memory_space=pltpu.SMEM)
    return pl.pallas_call(
        prepare_kernel,
        out_shape=(
            jax.ShapeDtypeStruct((2, ROWS, HD), BF),
            jax.ShapeDtypeStruct((ROWS, HD), BF),
            jax.ShapeDtypeStruct((NTILE, 8, TROWS), jnp.int32),
            jax.ShapeDtypeStruct((NTILE + NBLK,), jnp.int32),
        ),
        in_specs=[smem],
        out_specs=(vmem, vmem, vmem, smem),
        compiler_params=pltpu.CompilerParams(vmem_limit_bytes=12 << 20),
        name="prepare",
    )(ints)


AHEAD = 2 * HALF
MAXBEFORE = 3


def attend_kernel(core_ref, meta_ref, y_ref, kvo_ref, kdoc_ref, qdoc_ref, hi_ref, o_ref):
    core = core_ref[0]

    def half_pos(index):
        return 2 * index - (index & (QTR - 1))

    def query_tile(j, c):
        qrows = pl.ds(pl.multiple_of(j * TROWS, TROWS), TROWS)
        q = jnp.concatenate([y_ref[qrows, :HD], qdoc_ref[qrows, :]], axis=1)

        def run(before, after):
            start = pl.multiple_of((j - before) * TROWS, TROWS)
            count = (before + 1) * TROWS + after * AHEAD
            rows = pl.ds(start, count)
            own = (y_ref[rows, HD : 2 * HD], y_ref[rows, 2 * HD :], kdoc_ref[0, rows, :], core)
            other = (kvo_ref[rows, :HD], kvo_ref[rows, HD:], kdoc_ref[1, rows, :], 1 - core)
            scores = []
            tail = before * TROWS
            key_pos = half_pos(lax.broadcasted_iota(jnp.int32, (count - tail, TROWS), 0))
            for key, _, doc, parity in (own, other):
                s = lax.dot_general(
                    jnp.concatenate([key, doc], axis=1),
                    q,
                    (((1,), (1,)), ((), ())),
                    preferred_element_type=F32,
                )
                end = jnp.where(key_pos < hi_ref[j, :1, :] - parity * QTR, s[tail:], NEG)
                scores.append([s[:tail], end] if before else [end])
            peak = functools.reduce(
                jnp.maximum, [jnp.max(s, axis=0, keepdims=True) for part in scores for s in part]
            )
            l = jnp.zeros((1, TROWS), F32)
            acc = jnp.zeros((HD, TROWS), F32)
            for part, (_, value, _, _) in zip(scores, (own, other)):
                weights = []
                for s in part:
                    p = jnp.exp2((s - peak) * SCALE2)
                    l = l + jnp.sum(p, axis=0, keepdims=True)
                    weights.append(p.astype(BF))
                p = jnp.concatenate(weights, axis=0) if before else weights[0]
                acc = acc + lax.dot_general(
                    value, p, (((0,), (0,)), ((), ())), preferred_element_type=F32
                )
            out = jnp.transpose(acc / l).astype(BF)
            for b in range(TILE):
                slot = meta_ref[NTILE + j * TILE + b]
                chip = slot // CHIP_BLOCKS
                for u in range(2):
                    group = (slot % CHIP_BLOCKS) * 2 + u
                    o_ref[group // 3, chip, group % 3] = out[
                        b * HALF + u * QTR : b * HALF + (u + 1) * QTR
                    ]

        case = meta_ref[j]
        for before in range(MAXBEFORE + 1):
            for after in range(2):
                pl.when(case == 2 * before + after)(functools.partial(run, before, after))
        return c

    lax.fori_loop(0, NTILE, query_tile, 0)


def attend(core, meta, y, kvo, kdoc, qdoc, hi):
    vmem = pl.BlockSpec(memory_space=pltpu.VMEM)
    smem = pl.BlockSpec(memory_space=pltpu.SMEM)
    return pl.pallas_call(
        attend_kernel,
        out_shape=jax.ShapeDtypeStruct((2, NCTX, 3, QTR, HD), BF),
        in_specs=[smem, smem] + [vmem] * 5,
        out_specs=vmem,
        compiler_params=pltpu.CompilerParams(vmem_limit_bytes=14 << 20),
        name="attend",
    )(core, meta, y, kvo, kdoc, qdoc, hi)


SHARED = (512, 1024)
LOADS = 8
DIRECT = (256, 256)
CTX = ("y", "x")
NLINE = 4
PIECE = HEADS * HD // NLINE
PHEADS = PIECE // HD


def project_kernel(ids_ref, z_ref, zo_ref, w_ref, *refs):
    count = NLINE * len(SHARED) + len(DIRECT)
    sides = (refs[:count], refs[count : 2 * count])
    o_ref, a_ref, b_ref = refs[2 * count : 2 * count + 3]
    bufs, (acc_ref, w_buf, p_buf, sems) = refs[2 * count + 3 : -4], refs[-4:]
    core, t_own = ids_ref[0], ids_ref[1]
    half = w_ref.shape[1] // 2

    steps = []
    for side in range(2):
        first = (core if side == 0 else 1 - core) * half
        start, part = 0, 0
        for n, width in enumerate(SHARED + DIRECT):
            column = pl.ds(pl.multiple_of(first + start, HD), width)
            place = slice(side * half + start, side * half + start + width)
            rows = PIECE if n < len(SHARED) else HEADS * HD
            loads = []
            for m in range(HEADS * HD // rows):
                loads.append(
                    pltpu.make_async_copy(
                        sides[side][part],
                        p_buf.at[m * rows : (m + 1) * rows, place],
                        sems.at[side, part],
                    )
                )
                loads[-1].start()
                part += 1
            steps.append((side, n, column, place, loads))
            start += width

    w_loads = []
    rows = w_ref.shape[0] // LOADS
    for n in range(LOADS):
        part = slice(n * rows, (n + 1) * rows)
        w_loads.append(pltpu.make_async_copy(w_ref.at[part], w_buf.at[part], sems.at[2, n]))
        w_loads[-1].start()

    def head(ref, at, src, h):
        col = slice(at * HD, (at + 1) * HD)
        for g in range(3):
            row = pl.multiple_of(g * HALF + core * QTR, QTR)
            ref[pl.ds(row, QTR), col] = z_ref[src, core * HEADS + h, g]
            row = pl.multiple_of(g * HALF + (1 - core) * QTR, QTR)
            ref[pl.ds(row, QTR), col] = zo_ref[src, h, g]

    for h in range(HEADS):
        head(a_ref, h, t_own, h)
        head(b_ref.at[2], h, 1 - t_own, h)
    for side in range(2):
        for n in range(NLINE):
            piece = (ids_ref[2 + side] + n) & (NLINE - 1)
            for h in range(PHEADS):
                head(b_ref.at[side], n * PHEADS + h, 1 - t_own, piece * PHEADS + h)

    for side, n, _, place, loads in steps:
        for load in loads:
            load.wait()
        left = b_ref[side] if n < len(SHARED) else b_ref[2]
        acc_ref[:, place] = jnp.dot(left, p_buf[:, place], preferred_element_type=F32)
    for load in w_loads:
        load.wait()
    stores = []
    for side, n, column, place, _ in steps:
        acc = acc_ref[:, place] + jnp.dot(
            a_ref[...], w_buf[:, column], preferred_element_type=F32
        )
        buf = bufs[n].at[side]
        buf[...] = acc.astype(BF)
        store = pltpu.make_async_copy(buf, o_ref.at[:, column], sems.at[3 + side, n])
        store.start()
        stores.append(store)
    for store in stores:
        store.wait()


def project(ids, z, zo, w, mine, other):
    width = w.shape[1]
    depth = HEADS * HD
    rows = 3 * HALF
    parts = mine + other
    widths = SHARED + DIRECT
    vmem = pl.BlockSpec(memory_space=pltpu.VMEM)
    hbm = pl.BlockSpec(memory_space=pltpu.HBM)
    return pl.pallas_call(
        project_kernel,
        in_specs=[pl.BlockSpec(memory_space=pltpu.SMEM), vmem, vmem] + [hbm] * (1 + len(parts)),
        out_specs=hbm,
        out_shape=jax.ShapeDtypeStruct((rows, width), BF),
        scratch_shapes=[pltpu.VMEM((rows, depth), BF), pltpu.VMEM((3, rows, depth), BF)]
        + [pltpu.VMEM((2, rows, n), BF) for n in widths]
        + [
            pltpu.VMEM((rows, width), F32),
            pltpu.VMEM((depth, width), BF),
            pltpu.VMEM((depth, width), BF),
            pltpu.SemaphoreType.DMA((5, max(LOADS, len(mine)))),
        ],
        compiler_params=pltpu.CompilerParams(vmem_limit_bytes=32 << 20),
        name="project",
    )(ids, z, zo, w, *parts)


def pick_kernel(core_ref, z_ref, o_ref):
    o_ref[...] = z_ref[:, pl.ds((1 - core_ref[0]) * HEADS, HEADS)]


def pick(core, z):
    vmem = pl.BlockSpec(memory_space=pltpu.VMEM)
    return pl.pallas_call(
        pick_kernel,
        out_shape=jax.ShapeDtypeStruct((2, HEADS) + z.shape[2:], BF),
        in_specs=[pl.BlockSpec(memory_space=pltpu.SMEM), vmem],
        out_specs=vmem,
        compiler_params=pltpu.CompilerParams(vmem_limit_bytes=4 << 20),
        name="pick",
    )(core, z)


SWAP = [(0, 1), (1, 0)]


def swap(x):
    return lax.ppermute(x, "core", SWAP)


def in_hbm(x):
    return pltpu.with_memory_space_constraint(x, pltpu.HBM)


def after(values, *others):
    return lax.optimization_barrier((values,) + others)[0]


def along_line(x, step):
    pairs = []
    for y in range(NLINE):
        for x_at in range(NLINE):
            for core in range(2):
                to = (y, (x_at - step) % NLINE) if core == 0 else ((y - step) % NLINE, x_at)
                index = lambda y, x: (core * NLINE + y) * NLINE + x
                pairs.append((index(y, x_at), index(*to)))
    return lax.ppermute(x, ("core",) + CTX, pairs)


def shards(q, k, v, w, doc_lengths, spans, assignment):
    core = lax.axis_index("core").astype(jnp.int32)
    t_own = lax.axis_index("tensor").astype(jnp.int32)
    x_at = lax.axis_index("x").astype(jnp.int32)
    y_at = lax.axis_index("y").astype(jnp.int32)
    chip = y_at * NLINE + x_at

    across = [(a * 2 + b, (1 - a) * 2 + 1 - b) for a in range(2) for b in range(2)]
    from_z = lambda x: lax.ppermute(x, ("z_lo", "tensor"), across)
    half = w.shape[1] // 2
    line = jnp.where(core == 0, x_at, y_at)
    at = core * half
    fetched = []
    for width in SHARED:
        fetched.append(from_z(lax.dynamic_slice(w, (PIECE * line, at), (PIECE, width))))
        at += width
    direct = []
    for width in DIRECT:
        direct.append(lax.dynamic_slice(w, (0, at), (w.shape[0], width)))
        at += width
    first = from_z(after(direct[0], fetched[0]))
    share = lambda piece: [piece] + [along_line(piece, step) for step in (1, 2, 3)]
    early = share(fetched[0])

    ints = jnp.concatenate([doc_lengths, spans.reshape(-1), assignment])
    ints = jnp.where(chip // HEADS == core, ints, swap(ints))
    ints = jnp.concatenate([core[None], ints])

    q, k, v = (in_hbm(x) for x in (q, k, v))
    own, send = pack(core[None], q, k, v)
    recv = swap(send)
    x = merge(core[None], own, recv)
    y = lax.all_to_all(x, CTX, 0, 0, tiled=True).reshape(ROWS, 3 * HD)
    kdoc, qdoc, hi, meta = prepare(ints)
    y, kdoc, qdoc, hi, meta = lax.optimization_barrier((y, kdoc, qdoc, hi, meta))
    y, early, piece, first = lax.optimization_barrier((y, early, fetched[1], first))
    second = from_z(after(direct[1], first))
    kvo = swap(y[:, HD:])

    pieces = share(piece)
    att = attend(core[None], meta, y, kvo, kdoc, qdoc, hi)
    att, mine = lax.optimization_barrier((att, early + pieces + [first, second]))
    other = [swap(p) for p in mine]
    z = lax.all_to_all(
        att.reshape(2 * NCTX, 3, QTR, HD), ("tensor",) + CTX, 0, 0, tiled=True
    ).reshape(2, 2 * HEADS, 3, QTR, HD)
    zo = swap(pick(core[None], z))
    lines = jnp.where(core == 0, jnp.stack([x_at, y_at]), jnp.stack([y_at, x_at]))
    ids = jnp.concatenate([jnp.stack([core, t_own]), lines])
    mine, other = ([in_hbm(p) for p in side] for side in (mine, other))
    return project(ids, z, zo, in_hbm(w), mine, other)


def solution(mesh):
    fine = Mesh(
        mesh.devices.reshape(2, 2, NLINE, NLINE, 2), ("z_lo", "core", "y", "x", "tensor")
    )
    dp = ("z_lo", "core")
    rows = P(dp + CTX, "tensor")
    placed = (rows, rows, rows, P("tensor", None), P(dp), P(dp, None), P(dp))
    return jax.shard_map(
        shards,
        mesh=fine,
        in_specs=placed,
        out_specs=P(dp + CTX + ("tensor",), None),
        check_vma=False,
    )
```

```python
import functools
import math

import jax
import jax.numpy as jnp
from jax import lax
from jax.experimental import pallas as pl
from jax.experimental.pallas import tpu as pltpu
from jax.sharding import Mesh, PartitionSpec as P

HD = 128
QB = 128
QTR = QB // 4
HALF = QB // 2
NCTX = 16
CHIP_BLOCKS = 3
NBLK = NCTX * CHIP_BLOCKS
HEADS = 8
ROWS = NBLK * HALF
NDOC = 6
NSPAN = 31
TILE = 4
TROWS = TILE * HALF
TPOS = TILE * QB
NTILE = NBLK // TILE
SCALE2 = math.log2(math.e) / math.sqrt(HD)
NEG = -1e30
BF = jnp.bfloat16
F32 = jnp.float32


def pack_kernel(core_ref, q_hbm, k_hbm, v_hbm, own_ref, send_ref, buf, sems):
    core = core_ref[0]
    copies = []
    for block in range(CHIP_BLOCKS):
        rows = slice(block * QB, (block + 1) * QB)
        for a, ref in enumerate((q_hbm, k_hbm, v_hbm)):
            copy = pltpu.make_async_copy(ref.at[rows], buf.at[a, rows], sems.at[block, a])
            copy.start()
            copies.append(copy)
    for block in range(CHIP_BLOCKS):
        for a in range(3):
            copies[block * 3 + a].wait()
            for out_ref, parity in ((own_ref, core), (send_ref, 1 - core)):
                for group in (2 * block, 2 * block + 1):
                    start = pl.multiple_of(group * HALF + parity * QTR, QTR)
                    rows = buf[a, pl.ds(start, QTR), :]
                    for h in range(HEADS):
                        out_ref[
                            h, group * QTR : (group + 1) * QTR, a * HD : (a + 1) * HD
                        ] = rows[:, h * HD : (h + 1) * HD]


def pack(core, q, k, v):
    out = jax.ShapeDtypeStruct((HEADS, CHIP_BLOCKS * HALF, 3 * HD), BF)
    vmem = pl.BlockSpec(memory_space=pltpu.VMEM)
    hbm = pl.BlockSpec(memory_space=pltpu.HBM)
    return pl.pallas_call(
        pack_kernel,
        out_shape=(out, out),
        in_specs=[pl.BlockSpec(memory_space=pltpu.SMEM), hbm, hbm, hbm],
        out_specs=(vmem, vmem),
        scratch_shapes=[
            pltpu.VMEM((3,) + q.shape, BF),
            pltpu.SemaphoreType.DMA((CHIP_BLOCKS, 3)),
        ],
        compiler_params=pltpu.CompilerParams(vmem_limit_bytes=12 << 20),
        name="pack",
    )(core, q, k, v)


def merge_kernel(core_ref, own_ref, recv_ref, o_ref):
    core = core_ref[0]
    o_ref[pl.ds(core * HEADS, HEADS)] = own_ref[...]
    o_ref[pl.ds((1 - core) * HEADS, HEADS)] = recv_ref[...]


def merge(core, own, recv):
    vmem = pl.BlockSpec(memory_space=pltpu.VMEM)
    return pl.pallas_call(
        merge_kernel,
        out_shape=jax.ShapeDtypeStruct((2 * HEADS,) + own.shape[1:], BF),
        in_specs=[pl.BlockSpec(memory_space=pltpu.SMEM), vmem, vmem],
        out_specs=vmem,
        compiler_params=pltpu.CompilerParams(vmem_limit_bytes=12 << 20),
        name="merge",
    )(core, own, recv)


def prepare_kernel(ints_ref, kdoc_ref, qdoc_ref, hi_ref, meta_ref):
    core = ints_ref[0]
    spans_at = 1 + NDOC
    assign_at = spans_at + 2 * NSPAN

    def half_pos(index, parity):
        return 2 * index - (index & (QTR - 1)) + parity * QTR

    lane = lax.broadcasted_iota(jnp.int32, (8, HD), 1)
    starts, start = [], jnp.int32(0)
    first = jnp.zeros((8, HD), jnp.int32)
    last = jnp.zeros((8, HD), jnp.int32)
    for d in range(NDOC):
        end = start + ints_ref[1 + d]
        first = jnp.where(lane == d, start, first)
        last = jnp.where(lane == d, end, last)
        starts.append(start)
        start = end
    first, last = first[:1], last[:1]
    used = lane[:1] < NDOC
    for c in range(NCTX):
        rows = slice(c * CHIP_BLOCKS * HALF, (c + 1) * CHIP_BLOCKS * HALF)
        index = lax.broadcasted_iota(jnp.int32, (CHIP_BLOCKS * HALF, HD), 0)
        base = half_pos(index, 0) + c * CHIP_BLOCKS * QB
        for n, parity in enumerate((core, 1 - core)):
            pos = base + parity * QTR
            inside = (pos >= first) & (pos < last)
            kdoc_ref[n, rows, :] = jnp.where(inside, 1.0, 0.0).astype(BF)
            if n == 0:
                qdoc_ref[rows, :] = jnp.where(inside | ~used, 0.0, NEG).astype(BF)

    def query_tile(j, c):
        tile_first = j * TPOS
        pos = half_pos(lax.broadcasted_iota(jnp.int32, (8, TROWS), 1), core) + tile_first

        def one_span(s, hi):
            a = ints_ref[spans_at + 2 * s]
            b = ints_ref[spans_at + 2 * s + 1]
            return jnp.where((pos >= a) & (pos < b), b, hi)

        hi = lax.fori_loop(0, NSPAN, one_span, pos + 1, unroll=True)
        hi_ref[j] = hi - tile_first
        lo_first = jnp.int32(0)
        for d in range(NDOC):
            lo_first = jnp.where(tile_first >= starts[d], starts[d], lo_first)
        before = j - lo_first // TPOS
        after = jnp.where(jnp.max(hi) > tile_first + TPOS, 1, 0)
        after = jnp.where(j == NTILE - 1, 0, after)
        meta_ref[j] = 2 * before + after
        return c

    lax.fori_loop(0, NTILE, query_tile, 0)

    def invert(j, c):
        meta_ref[NTILE + ints_ref[assign_at + j]] = j
        return c

    lax.fori_loop(0, NBLK, invert, 0)


def prepare(ints):
    vmem = pl.BlockSpec(memory_space=pltpu.VMEM)
    smem = pl.BlockSpec(memory_space=pltpu.SMEM)
    return pl.pallas_call(
        prepare_kernel,
        out_shape=(
            jax.ShapeDtypeStruct((2, ROWS, HD), BF),
            jax.ShapeDtypeStruct((ROWS, HD), BF),
            jax.ShapeDtypeStruct((NTILE, 8, TROWS), jnp.int32),
            jax.ShapeDtypeStruct((NTILE + NBLK,), jnp.int32),
        ),
        in_specs=[smem],
        out_specs=(vmem, vmem, vmem, smem),
        compiler_params=pltpu.CompilerParams(vmem_limit_bytes=12 << 20),
        name="prepare",
    )(ints)


AHEAD = 2 * HALF
MAXBEFORE = 3


def attend_kernel(core_ref, meta_ref, y_ref, kvo_ref, kdoc_ref, qdoc_ref, hi_ref, o_ref):
    core = core_ref[0]

    def half_pos(index):
        return 2 * index - (index & (QTR - 1))

    def query_tile(j, c):
        qrows = pl.ds(pl.multiple_of(j * TROWS, TROWS), TROWS)
        q = jnp.concatenate([y_ref[qrows, :HD], qdoc_ref[qrows, :]], axis=1)

        def run(before, after):
            start = pl.multiple_of((j - before) * TROWS, TROWS)
            count = (before + 1) * TROWS + after * AHEAD
            rows = pl.ds(start, count)
            own = (y_ref[rows, HD : 2 * HD], y_ref[rows, 2 * HD :], kdoc_ref[0, rows, :], core)
            other = (kvo_ref[rows, :HD], kvo_ref[rows, HD:], kdoc_ref[1, rows, :], 1 - core)
            scores = []
            tail = before * TROWS
            key_pos = half_pos(lax.broadcasted_iota(jnp.int32, (count - tail, TROWS), 0))
            for key, _, doc, parity in (own, other):
                s = lax.dot_general(
                    jnp.concatenate([key, doc], axis=1),
                    q,
                    (((1,), (1,)), ((), ())),
                    preferred_element_type=F32,
                )
                end = jnp.where(key_pos < hi_ref[j, :1, :] - parity * QTR, s[tail:], NEG)
                scores.append([s[:tail], end] if before else [end])
            peak = functools.reduce(
                jnp.maximum, [jnp.max(s, axis=0, keepdims=True) for part in scores for s in part]
            )
            l = jnp.zeros((1, TROWS), F32)
            acc = jnp.zeros((HD, TROWS), F32)
            for part, (_, value, _, _) in zip(scores, (own, other)):
                weights = []
                for s in part:
                    p = jnp.exp2((s - peak) * SCALE2)
                    l = l + jnp.sum(p, axis=0, keepdims=True)
                    weights.append(p.astype(BF))
                p = jnp.concatenate(weights, axis=0) if before else weights[0]
                acc = acc + lax.dot_general(
                    value, p, (((0,), (0,)), ((), ())), preferred_element_type=F32
                )
            out = jnp.transpose(acc / l).astype(BF)
            for b in range(TILE):
                slot = meta_ref[NTILE + j * TILE + b]
                chip = slot // CHIP_BLOCKS
                for u in range(2):
                    group = (slot % CHIP_BLOCKS) * 2 + u
                    o_ref[group // 3, chip, group % 3] = out[
                        b * HALF + u * QTR : b * HALF + (u + 1) * QTR
                    ]

        case = meta_ref[j]
        for before in range(MAXBEFORE + 1):
            for after in range(2):
                pl.when(case == 2 * before + after)(functools.partial(run, before, after))
        return c

    lax.fori_loop(0, NTILE, query_tile, 0)


def attend(core, meta, y, kvo, kdoc, qdoc, hi):
    vmem = pl.BlockSpec(memory_space=pltpu.VMEM)
    smem = pl.BlockSpec(memory_space=pltpu.SMEM)
    return pl.pallas_call(
        attend_kernel,
        out_shape=jax.ShapeDtypeStruct((2, NCTX, 3, QTR, HD), BF),
        in_specs=[smem, smem] + [vmem] * 5,
        out_specs=vmem,
        compiler_params=pltpu.CompilerParams(vmem_limit_bytes=14 << 20),
        name="attend",
    )(core, meta, y, kvo, kdoc, qdoc, hi)


SHARED = (256, 1280)
LOADS = 8
DIRECT = (256, 256)
CTX = ("y", "x")
NLINE = 4
PIECE = HEADS * HD // NLINE
PHEADS = PIECE // HD


def project_kernel(ids_ref, z_ref, zo_ref, w_ref, *refs):
    count = NLINE * len(SHARED) + len(DIRECT)
    sides = (refs[:count], refs[count : 2 * count])
    o_ref, a_ref, b_ref = refs[2 * count : 2 * count + 3]
    bufs, (acc_ref, w_buf, p_buf, sems) = refs[2 * count + 3 : -4], refs[-4:]
    core, t_own = ids_ref[0], ids_ref[1]
    half = w_ref.shape[1] // 2

    steps = []
    for side in range(2):
        first = (core if side == 0 else 1 - core) * half
        start, part = 0, 0
        for n, width in enumerate(SHARED + DIRECT):
            column = pl.ds(pl.multiple_of(first + start, HD), width)
            place = slice(side * half + start, side * half + start + width)
            rows = PIECE if n < len(SHARED) else HEADS * HD
            loads = []
            for m in range(HEADS * HD // rows):
                loads.append(
                    pltpu.make_async_copy(
                        sides[side][part],
                        p_buf.at[m * rows : (m + 1) * rows, place],
                        sems.at[side, part],
                    )
                )
                loads[-1].start()
                part += 1
            steps.append((side, n, column, place, loads))
            start += width

    w_loads = []
    rows = w_ref.shape[0] // LOADS
    for n in range(LOADS):
        part = slice(n * rows, (n + 1) * rows)
        w_loads.append(pltpu.make_async_copy(w_ref.at[part], w_buf.at[part], sems.at[2, n]))
        w_loads[-1].start()

    def head(ref, at, src, h):
        col = slice(at * HD, (at + 1) * HD)
        for g in range(3):
            row = pl.multiple_of(g * HALF + core * QTR, QTR)
            ref[pl.ds(row, QTR), col] = z_ref[src, core * HEADS + h, g]
            row = pl.multiple_of(g * HALF + (1 - core) * QTR, QTR)
            ref[pl.ds(row, QTR), col] = zo_ref[src, h, g]

    for h in range(HEADS):
        head(a_ref, h, t_own, h)
        head(b_ref.at[2], h, 1 - t_own, h)
    for side in range(2):
        for n in range(NLINE):
            piece = (ids_ref[2 + side] + n) & (NLINE - 1)
            for h in range(PHEADS):
                head(b_ref.at[side], n * PHEADS + h, 1 - t_own, piece * PHEADS + h)

    for side, n, _, place, loads in steps:
        for load in loads:
            load.wait()
        left = b_ref[side] if n < len(SHARED) else b_ref[2]
        acc_ref[:, place] = jnp.dot(left, p_buf[:, place], preferred_element_type=F32)
    for load in w_loads:
        load.wait()
    stores = []
    for side, n, column, place, _ in steps:
        acc = acc_ref[:, place] + jnp.dot(
            a_ref[...], w_buf[:, column], preferred_element_type=F32
        )
        buf = bufs[n].at[side]
        buf[...] = acc.astype(BF)
        store = pltpu.make_async_copy(buf, o_ref.at[:, column], sems.at[3 + side, n])
        store.start()
        stores.append(store)
    for store in stores:
        store.wait()


def project(ids, z, zo, w, mine, other):
    width = w.shape[1]
    depth = HEADS * HD
    rows = 3 * HALF
    parts = mine + other
    widths = SHARED + DIRECT
    vmem = pl.BlockSpec(memory_space=pltpu.VMEM)
    hbm = pl.BlockSpec(memory_space=pltpu.HBM)
    return pl.pallas_call(
        project_kernel,
        in_specs=[pl.BlockSpec(memory_space=pltpu.SMEM), vmem, vmem] + [hbm] * (1 + len(parts)),
        out_specs=hbm,
        out_shape=jax.ShapeDtypeStruct((rows, width), BF),
        scratch_shapes=[pltpu.VMEM((rows, depth), BF), pltpu.VMEM((3, rows, depth), BF)]
        + [pltpu.VMEM((2, rows, n), BF) for n in widths]
        + [
            pltpu.VMEM((rows, width), F32),
            pltpu.VMEM((depth, width), BF),
            pltpu.VMEM((depth, width), BF),
            pltpu.SemaphoreType.DMA((5, max(LOADS, len(mine)))),
        ],
        compiler_params=pltpu.CompilerParams(vmem_limit_bytes=32 << 20),
        name="project",
    )(ids, z, zo, w, *parts)


def pick_kernel(core_ref, z_ref, o_ref):
    o_ref[...] = z_ref[:, pl.ds((1 - core_ref[0]) * HEADS, HEADS)]


def pick(core, z):
    vmem = pl.BlockSpec(memory_space=pltpu.VMEM)
    return pl.pallas_call(
        pick_kernel,
        out_shape=jax.ShapeDtypeStruct((2, HEADS) + z.shape[2:], BF),
        in_specs=[pl.BlockSpec(memory_space=pltpu.SMEM), vmem],
        out_specs=vmem,
        compiler_params=pltpu.CompilerParams(vmem_limit_bytes=4 << 20),
        name="pick",
    )(core, z)


SWAP = [(0, 1), (1, 0)]


def swap(x):
    return lax.ppermute(x, "core", SWAP)


def in_hbm(x):
    return pltpu.with_memory_space_constraint(x, pltpu.HBM)


def after(values, *others):
    return lax.optimization_barrier((values,) + others)[0]


def along_line(x, step):
    pairs = []
    for y in range(NLINE):
        for x_at in range(NLINE):
            for core in range(2):
                to = (y, (x_at - step) % NLINE) if core == 0 else ((y - step) % NLINE, x_at)
                index = lambda y, x: (core * NLINE + y) * NLINE + x
                pairs.append((index(y, x_at), index(*to)))
    return lax.ppermute(x, ("core",) + CTX, pairs)


def shards(q, k, v, w, doc_lengths, spans, assignment):
    core = lax.axis_index("core").astype(jnp.int32)
    t_own = lax.axis_index("tensor").astype(jnp.int32)
    x_at = lax.axis_index("x").astype(jnp.int32)
    y_at = lax.axis_index("y").astype(jnp.int32)
    chip = y_at * NLINE + x_at

    across = [(a * 2 + b, (1 - a) * 2 + 1 - b) for a in range(2) for b in range(2)]
    from_z = lambda x: lax.ppermute(x, ("z_lo", "tensor"), across)
    half = w.shape[1] // 2
    line = jnp.where(core == 0, x_at, y_at)
    at = core * half
    fetched = []
    for width in SHARED:
        fetched.append(from_z(lax.dynamic_slice(w, (PIECE * line, at), (PIECE, width))))
        at += width
    direct = []
    for width in DIRECT:
        direct.append(lax.dynamic_slice(w, (0, at), (w.shape[0], width)))
        at += width
    first = from_z(after(direct[0], fetched[0]))
    share = lambda piece: [piece] + [along_line(piece, step) for step in (1, 2, 3)]
    early = share(fetched[0])

    ints = jnp.concatenate([doc_lengths, spans.reshape(-1), assignment])
    ints = jnp.where(chip // HEADS == core, ints, swap(ints))
    ints = jnp.concatenate([core[None], ints])

    q, k, v = (in_hbm(x) for x in (q, k, v))
    own, send = pack(core[None], q, k, v)
    recv = swap(send)
    x = merge(core[None], own, recv)
    y = lax.all_to_all(x, CTX, 0, 0, tiled=True).reshape(ROWS, 3 * HD)
    kdoc, qdoc, hi, meta = prepare(ints)
    y, kdoc, qdoc, hi, meta = lax.optimization_barrier((y, kdoc, qdoc, hi, meta))
    y, early, piece, first = lax.optimization_barrier((y, early, fetched[1], first))
    second = from_z(after(direct[1], first))
    kvo = swap(y[:, HD:])

    pieces = share(piece)
    att = attend(core[None], meta, y, kvo, kdoc, qdoc, hi)
    att, mine = lax.optimization_barrier((att, early + pieces + [first, second]))
    other = [swap(p) for p in mine]
    z = lax.all_to_all(
        att.reshape(2 * NCTX, 3, QTR, HD), ("tensor",) + CTX, 0, 0, tiled=True
    ).reshape(2, 2 * HEADS, 3, QTR, HD)
    zo = swap(pick(core[None], z))
    lines = jnp.where(core == 0, jnp.stack([x_at, y_at]), jnp.stack([y_at, x_at]))
    ids = jnp.concatenate([jnp.stack([core, t_own]), lines])
    mine, other = ([in_hbm(p) for p in side] for side in (mine, other))
    return project(ids, z, zo, in_hbm(w), mine, other)


def solution(mesh):
    fine = Mesh(
        mesh.devices.reshape(2, 2, NLINE, NLINE, 2), ("z_lo", "core", "y", "x", "tensor")
    )
    dp = ("z_lo", "core")
    rows = P(dp + CTX, "tensor")
    placed = (rows, rows, rows, P("tensor", None), P(dp), P(dp, None), P(dp))
    return jax.shard_map(
        shards,
        mesh=fine,
        in_specs=placed,
        out_specs=P(dp + CTX + ("tensor",), None),
        check_vma=False,
    )
```

```python
import functools
import math

import jax
import jax.numpy as jnp
from jax import lax
from jax.experimental import pallas as pl
from jax.experimental.pallas import tpu as pltpu
from jax.sharding import Mesh, PartitionSpec as P

HD = 128
QB = 128
QTR = QB // 4
HALF = QB // 2
NCTX = 16
CHIP_BLOCKS = 3
NBLK = NCTX * CHIP_BLOCKS
HEADS = 8
ROWS = NBLK * HALF
NDOC = 6
NSPAN = 31
TILE = 4
TROWS = TILE * HALF
TPOS = TILE * QB
NTILE = NBLK // TILE
SCALE2 = math.log2(math.e) / math.sqrt(HD)
NEG = -1e30
BF = jnp.bfloat16
F32 = jnp.float32


def pack_kernel(core_ref, q_hbm, k_hbm, v_hbm, own_ref, send_ref, buf, sems):
    core = core_ref[0]
    copies = []
    for block in range(CHIP_BLOCKS):
        rows = slice(block * QB, (block + 1) * QB)
        for a, ref in enumerate((q_hbm, k_hbm, v_hbm)):
            copy = pltpu.make_async_copy(ref.at[rows], buf.at[a, rows], sems.at[block, a])
            copy.start()
            copies.append(copy)
    for block in range(CHIP_BLOCKS):
        for a in range(3):
            copies[block * 3 + a].wait()
            for out_ref, parity in ((own_ref, core), (send_ref, 1 - core)):
                for group in (2 * block, 2 * block + 1):
                    start = pl.multiple_of(group * HALF + parity * QTR, QTR)
                    rows = buf[a, pl.ds(start, QTR), :]
                    for h in range(HEADS):
                        out_ref[
                            h, group * QTR : (group + 1) * QTR, a * HD : (a + 1) * HD
                        ] = rows[:, h * HD : (h + 1) * HD]


def pack(core, q, k, v):
    out = jax.ShapeDtypeStruct((HEADS, CHIP_BLOCKS * HALF, 3 * HD), BF)
    vmem = pl.BlockSpec(memory_space=pltpu.VMEM)
    hbm = pl.BlockSpec(memory_space=pltpu.HBM)
    return pl.pallas_call(
        pack_kernel,
        out_shape=(out, out),
        in_specs=[pl.BlockSpec(memory_space=pltpu.SMEM), hbm, hbm, hbm],
        out_specs=(vmem, vmem),
        scratch_shapes=[
            pltpu.VMEM((3,) + q.shape, BF),
            pltpu.SemaphoreType.DMA((CHIP_BLOCKS, 3)),
        ],
        compiler_params=pltpu.CompilerParams(vmem_limit_bytes=12 << 20),
        name="pack",
    )(core, q, k, v)


def merge_kernel(core_ref, own_ref, recv_ref, o_ref):
    core = core_ref[0]
    o_ref[pl.ds(core * HEADS, HEADS)] = own_ref[...]
    o_ref[pl.ds((1 - core) * HEADS, HEADS)] = recv_ref[...]


def merge(core, own, recv):
    vmem = pl.BlockSpec(memory_space=pltpu.VMEM)
    return pl.pallas_call(
        merge_kernel,
        out_shape=jax.ShapeDtypeStruct((2 * HEADS,) + own.shape[1:], BF),
        in_specs=[pl.BlockSpec(memory_space=pltpu.SMEM), vmem, vmem],
        out_specs=vmem,
        compiler_params=pltpu.CompilerParams(vmem_limit_bytes=12 << 20),
        name="merge",
    )(core, own, recv)


def prepare_kernel(ints_ref, kdoc_ref, qdoc_ref, hi_ref, meta_ref):
    core = ints_ref[0]
    spans_at = 1 + NDOC
    assign_at = spans_at + 2 * NSPAN

    def half_pos(index, parity):
        return 2 * index - (index & (QTR - 1)) + parity * QTR

    lane = lax.broadcasted_iota(jnp.int32, (8, HD), 1)
    starts, start = [], jnp.int32(0)
    first = jnp.zeros((8, HD), jnp.int32)
    last = jnp.zeros((8, HD), jnp.int32)
    for d in range(NDOC):
        end = start + ints_ref[1 + d]
        first = jnp.where(lane == d, start, first)
        last = jnp.where(lane == d, end, last)
        starts.append(start)
        start = end
    first, last = first[:1], last[:1]
    used = lane[:1] < NDOC
    for c in range(NCTX):
        rows = slice(c * CHIP_BLOCKS * HALF, (c + 1) * CHIP_BLOCKS * HALF)
        index = lax.broadcasted_iota(jnp.int32, (CHIP_BLOCKS * HALF, HD), 0)
        base = half_pos(index, 0) + c * CHIP_BLOCKS * QB
        for n, parity in enumerate((core, 1 - core)):
            pos = base + parity * QTR
            inside = (pos >= first) & (pos < last)
            kdoc_ref[n, rows, :] = jnp.where(inside, 1.0, 0.0).astype(BF)
            if n == 0:
                qdoc_ref[rows, :] = jnp.where(inside | ~used, 0.0, NEG).astype(BF)

    def query_tile(j, c):
        tile_first = j * TPOS
        pos = half_pos(lax.broadcasted_iota(jnp.int32, (8, TROWS), 1), core) + tile_first

        def one_span(s, hi):
            a = ints_ref[spans_at + 2 * s]
            b = ints_ref[spans_at + 2 * s + 1]
            return jnp.where((pos >= a) & (pos < b), b, hi)

        hi = lax.fori_loop(0, NSPAN, one_span, pos + 1, unroll=True)
        hi_ref[j] = hi - tile_first
        lo_first = jnp.int32(0)
        for d in range(NDOC):
            lo_first = jnp.where(tile_first >= starts[d], starts[d], lo_first)
        before = j - lo_first // TPOS
        after = jnp.where(jnp.max(hi) > tile_first + TPOS, 1, 0)
        after = jnp.where(j == NTILE - 1, 0, after)
        meta_ref[j] = 2 * before + after
        return c

    lax.fori_loop(0, NTILE, query_tile, 0)

    def invert(j, c):
        meta_ref[NTILE + ints_ref[assign_at + j]] = j
        return c

    lax.fori_loop(0, NBLK, invert, 0)


def prepare(ints):
    vmem = pl.BlockSpec(memory_space=pltpu.VMEM)
    smem = pl.BlockSpec(memory_space=pltpu.SMEM)
    return pl.pallas_call(
        prepare_kernel,
        out_shape=(
            jax.ShapeDtypeStruct((2, ROWS, HD), BF),
            jax.ShapeDtypeStruct((ROWS, HD), BF),
            jax.ShapeDtypeStruct((NTILE, 8, TROWS), jnp.int32),
            jax.ShapeDtypeStruct((NTILE + NBLK,), jnp.int32),
        ),
        in_specs=[smem],
        out_specs=(vmem, vmem, vmem, smem),
        compiler_params=pltpu.CompilerParams(vmem_limit_bytes=12 << 20),
        name="prepare",
    )(ints)


AHEAD = 2 * HALF
MAXBEFORE = 3


def attend_kernel(core_ref, meta_ref, y_ref, kvo_ref, kdoc_ref, qdoc_ref, hi_ref, o_ref):
    core = core_ref[0]

    def half_pos(index):
        return 2 * index - (index & (QTR - 1))

    def query_tile(j, c):
        qrows = pl.ds(pl.multiple_of(j * TROWS, TROWS), TROWS)
        q = jnp.concatenate([y_ref[qrows, :HD], qdoc_ref[qrows, :]], axis=1)

        def run(before, after):
            start = pl.multiple_of((j - before) * TROWS, TROWS)
            count = (before + 1) * TROWS + after * AHEAD
            rows = pl.ds(start, count)
            own = (y_ref[rows, HD : 2 * HD], y_ref[rows, 2 * HD :], kdoc_ref[0, rows, :], core)
            other = (kvo_ref[rows, :HD], kvo_ref[rows, HD:], kdoc_ref[1, rows, :], 1 - core)
            scores = []
            tail = before * TROWS
            key_pos = half_pos(lax.broadcasted_iota(jnp.int32, (count - tail, TROWS), 0))
            for key, _, doc, parity in (own, other):
                s = lax.dot_general(
                    jnp.concatenate([key, doc], axis=1),
                    q,
                    (((1,), (1,)), ((), ())),
                    preferred_element_type=F32,
                )
                end = jnp.where(key_pos < hi_ref[j, :1, :] - parity * QTR, s[tail:], NEG)
                scores.append([s[:tail], end] if before else [end])
            peak = functools.reduce(
                jnp.maximum, [jnp.max(s, axis=0, keepdims=True) for part in scores for s in part]
            )
            l = jnp.zeros((1, TROWS), F32)
            acc = jnp.zeros((HD, TROWS), F32)
            for part, (_, value, _, _) in zip(scores, (own, other)):
                weights = []
                for s in part:
                    p = jnp.exp2((s - peak) * SCALE2)
                    l = l + jnp.sum(p, axis=0, keepdims=True)
                    weights.append(p.astype(BF))
                p = jnp.concatenate(weights, axis=0) if before else weights[0]
                acc = acc + lax.dot_general(
                    value, p, (((0,), (0,)), ((), ())), preferred_element_type=F32
                )
            out = jnp.transpose(acc * (1.0 / l)).astype(BF)
            for b in range(TILE):
                slot = meta_ref[NTILE + j * TILE + b]
                chip = slot // CHIP_BLOCKS
                for u in range(2):
                    group = (slot % CHIP_BLOCKS) * 2 + u
                    o_ref[group // 3, chip, group % 3] = out[
                        b * HALF + u * QTR : b * HALF + (u + 1) * QTR
                    ]

        case = meta_ref[j]
        for before in range(MAXBEFORE + 1):
            for after in range(2):
                pl.when(case == 2 * before + after)(functools.partial(run, before, after))
        return c

    lax.fori_loop(0, NTILE, query_tile, 0)


def attend(core, meta, y, kvo, kdoc, qdoc, hi):
    vmem = pl.BlockSpec(memory_space=pltpu.VMEM)
    smem = pl.BlockSpec(memory_space=pltpu.SMEM)
    return pl.pallas_call(
        attend_kernel,
        out_shape=jax.ShapeDtypeStruct((2, NCTX, 3, QTR, HD), BF),
        in_specs=[smem, smem] + [vmem] * 5,
        out_specs=vmem,
        compiler_params=pltpu.CompilerParams(vmem_limit_bytes=14 << 20),
        name="attend",
    )(core, meta, y, kvo, kdoc, qdoc, hi)


SHARED = (256, 1280)
LOADS = 8
DIRECT = (256, 256)
CTX = ("y", "x")
NLINE = 4
PIECE = HEADS * HD // NLINE
PHEADS = PIECE // HD


def project_kernel(ids_ref, z_ref, zo_ref, w_ref, *refs):
    count = NLINE * len(SHARED) + len(DIRECT)
    sides = (refs[:count], refs[count : 2 * count])
    o_ref, a_ref, b_ref = refs[2 * count : 2 * count + 3]
    bufs, (acc_ref, w_buf, p_buf, sems) = refs[2 * count + 3 : -4], refs[-4:]
    core, t_own = ids_ref[0], ids_ref[1]
    half = w_ref.shape[1] // 2

    steps = []
    for side in range(2):
        first = (core if side == 0 else 1 - core) * half
        start, part = 0, 0
        for n, width in enumerate(SHARED + DIRECT):
            column = pl.ds(pl.multiple_of(first + start, HD), width)
            place = slice(side * half + start, side * half + start + width)
            rows = PIECE if n < len(SHARED) else HEADS * HD
            loads = []
            for m in range(HEADS * HD // rows):
                loads.append(
                    pltpu.make_async_copy(
                        sides[side][part],
                        p_buf.at[m * rows : (m + 1) * rows, place],
                        sems.at[side, part],
                    )
                )
                loads[-1].start()
                part += 1
            steps.append((side, n, column, place, loads))
            start += width

    w_loads = []
    rows = w_ref.shape[0] // LOADS
    for n in range(LOADS):
        part = slice(n * rows, (n + 1) * rows)
        w_loads.append(pltpu.make_async_copy(w_ref.at[part], w_buf.at[part], sems.at[2, n]))
        w_loads[-1].start()

    def head(ref, at, src, h):
        col = slice(at * HD, (at + 1) * HD)
        for g in range(3):
            row = pl.multiple_of(g * HALF + core * QTR, QTR)
            ref[pl.ds(row, QTR), col] = z_ref[src, core * HEADS + h, g]
            row = pl.multiple_of(g * HALF + (1 - core) * QTR, QTR)
            ref[pl.ds(row, QTR), col] = zo_ref[src, h, g]

    for h in range(HEADS):
        head(a_ref, h, t_own, h)
        head(b_ref.at[2], h, 1 - t_own, h)
    for side in range(2):
        for n in range(NLINE):
            piece = (ids_ref[2 + side] + n) & (NLINE - 1)
            for h in range(PHEADS):
                head(b_ref.at[side], n * PHEADS + h, 1 - t_own, piece * PHEADS + h)

    for side, n, _, place, loads in steps:
        for load in loads:
            load.wait()
        left = b_ref[side] if n < len(SHARED) else b_ref[2]
        acc_ref[:, place] = jnp.dot(left, p_buf[:, place], preferred_element_type=F32)
    for load in w_loads:
        load.wait()
    stores = []
    for side, n, column, place, _ in steps:
        acc = acc_ref[:, place] + jnp.dot(
            a_ref[...], w_buf[:, column], preferred_element_type=F32
        )
        buf = bufs[n].at[side]
        buf[...] = acc.astype(BF)
        store = pltpu.make_async_copy(buf, o_ref.at[:, column], sems.at[3 + side, n])
        store.start()
        stores.append(store)
    for store in stores:
        store.wait()


def project(ids, z, zo, w, mine, other):
    width = w.shape[1]
    depth = HEADS * HD
    rows = 3 * HALF
    parts = mine + other
    widths = SHARED + DIRECT
    vmem = pl.BlockSpec(memory_space=pltpu.VMEM)
    hbm = pl.BlockSpec(memory_space=pltpu.HBM)
    return pl.pallas_call(
        project_kernel,
        in_specs=[pl.BlockSpec(memory_space=pltpu.SMEM), vmem, vmem] + [hbm] * (1 + len(parts)),
        out_specs=hbm,
        out_shape=jax.ShapeDtypeStruct((rows, width), BF),
        scratch_shapes=[pltpu.VMEM((rows, depth), BF), pltpu.VMEM((3, rows, depth), BF)]
        + [pltpu.VMEM((2, rows, n), BF) for n in widths]
        + [
            pltpu.VMEM((rows, width), F32),
            pltpu.VMEM((depth, width), BF),
            pltpu.VMEM((depth, width), BF),
            pltpu.SemaphoreType.DMA((5, max(LOADS, len(mine)))),
        ],
        compiler_params=pltpu.CompilerParams(vmem_limit_bytes=32 << 20),
        name="project",
    )(ids, z, zo, w, *parts)


def pick_kernel(core_ref, z_ref, o_ref):
    o_ref[...] = z_ref[:, pl.ds((1 - core_ref[0]) * HEADS, HEADS)]


def pick(core, z):
    vmem = pl.BlockSpec(memory_space=pltpu.VMEM)
    return pl.pallas_call(
        pick_kernel,
        out_shape=jax.ShapeDtypeStruct((2, HEADS) + z.shape[2:], BF),
        in_specs=[pl.BlockSpec(memory_space=pltpu.SMEM), vmem],
        out_specs=vmem,
        compiler_params=pltpu.CompilerParams(vmem_limit_bytes=4 << 20),
        name="pick",
    )(core, z)


SWAP = [(0, 1), (1, 0)]


def swap(x):
    return lax.ppermute(x, "core", SWAP)


def in_hbm(x):
    return pltpu.with_memory_space_constraint(x, pltpu.HBM)


def after(values, *others):
    return lax.optimization_barrier((values,) + others)[0]


def along_line(x, step):
    pairs = []
    for y in range(NLINE):
        for x_at in range(NLINE):
            for core in range(2):
                to = (y, (x_at - step) % NLINE) if core == 0 else ((y - step) % NLINE, x_at)
                index = lambda y, x: (core * NLINE + y) * NLINE + x
                pairs.append((index(y, x_at), index(*to)))
    return lax.ppermute(x, ("core",) + CTX, pairs)


def shards(q, k, v, w, doc_lengths, spans, assignment):
    core = lax.axis_index("core").astype(jnp.int32)
    t_own = lax.axis_index("tensor").astype(jnp.int32)
    x_at = lax.axis_index("x").astype(jnp.int32)
    y_at = lax.axis_index("y").astype(jnp.int32)
    chip = y_at * NLINE + x_at

    across = [(a * 2 + b, (1 - a) * 2 + 1 - b) for a in range(2) for b in range(2)]
    from_z = lambda x: lax.ppermute(x, ("z_lo", "tensor"), across)
    half = w.shape[1] // 2
    line = jnp.where(core == 0, x_at, y_at)
    at = core * half
    fetched = []
    for width in SHARED:
        fetched.append(from_z(lax.dynamic_slice(w, (PIECE * line, at), (PIECE, width))))
        at += width
    direct = []
    for width in DIRECT:
        direct.append(lax.dynamic_slice(w, (0, at), (w.shape[0], width)))
        at += width
    first = from_z(after(direct[0], fetched[0]))
    share = lambda piece: [piece] + [along_line(piece, step) for step in (1, 2, 3)]
    early = share(fetched[0])

    ints = jnp.concatenate([doc_lengths, spans.reshape(-1), assignment])
    ints = jnp.where(chip // HEADS == core, ints, swap(ints))
    ints = jnp.concatenate([core[None], ints])

    q, k, v = (in_hbm(x) for x in (q, k, v))
    own, send = pack(core[None], q, k, v)
    recv = swap(send)
    x = merge(core[None], own, recv)
    y = lax.all_to_all(x, CTX, 0, 0, tiled=True).reshape(ROWS, 3 * HD)
    kdoc, qdoc, hi, meta = prepare(ints)
    y, kdoc, qdoc, hi, meta = lax.optimization_barrier((y, kdoc, qdoc, hi, meta))
    y, early, piece, first = lax.optimization_barrier((y, early, fetched[1], first))
    second = from_z(after(direct[1], first))
    kvo = swap(y[:, HD:])

    pieces = share(piece)
    att = attend(core[None], meta, y, kvo, kdoc, qdoc, hi)
    att, mine = lax.optimization_barrier((att, early + pieces + [first, second]))
    other = [swap(p) for p in mine]
    z = lax.all_to_all(
        att.reshape(2 * NCTX, 3, QTR, HD), ("tensor",) + CTX, 0, 0, tiled=True
    ).reshape(2, 2 * HEADS, 3, QTR, HD)
    zo = swap(pick(core[None], z))
    lines = jnp.where(core == 0, jnp.stack([x_at, y_at]), jnp.stack([y_at, x_at]))
    ids = jnp.concatenate([jnp.stack([core, t_own]), lines])
    mine, other = ([in_hbm(p) for p in side] for side in (mine, other))
    return project(ids, z, zo, in_hbm(w), mine, other)


def solution(mesh):
    fine = Mesh(
        mesh.devices.reshape(2, 2, NLINE, NLINE, 2), ("z_lo", "core", "y", "x", "tensor")
    )
    dp = ("z_lo", "core")
    rows = P(dp + CTX, "tensor")
    placed = (rows, rows, rows, P("tensor", None), P(dp), P(dp, None), P(dp))
    return jax.shard_map(
        shards,
        mesh=fine,
        in_specs=placed,
        out_specs=P(dp + CTX + ("tensor",), None),
        check_vma=False,
    )
```
